256 devices in a mesh: row: 64 (over z, y, core), col: 4 (over x).
Axes of the slice: x: 4, y: 4, z: 8, core: 2. Of those that a mesh axis runs over, the one named last changes fastest.
Arguments:
- row_embed: float32 [65536, 512], P(('row', 'col')), may hold values from -1.5 to 1.5
- row_accum: float32 [65536, 512], P(('row', 'col')), may hold values from 0.001 to 0.01
- col_embed: float32 [4, 4096, 512], P('col', 'row'), may hold values from -1.5 to 1.5
- col_accum: float32 [4, 4096, 512], P('col', 'row'), may hold values from 0.001 to 0.01
- col_freq: int32 [4, 4096], P('col'), may hold values from 1000 to 29999
- row_freq: int32 [65536], P('row'), may hold values from 1000 to 29999
- block_cols: int32 [64, 4, 2], P('row', 'col'), may hold values from 0 to 3, all different within a row
- counts: int32 [64, 4, 2, 1024, 1024], P('row', 'col'), may hold values from 0 to 1024
- excluded: int32 [512], replicated, may hold values from 0 to 65535
- log_total: float32 [], replicated, may hold values from 15 to 19
Outputs:
- row_embed_new: float32 [65536, 512], P(('row', 'col'))
- row_accum_new: float32 [65536, 512], P(('row', 'col'))
- col_embed_new: float32 [4, 4096, 512], P('col', 'row')
- col_accum_new: float32 [4, 4096, 512], P('col', 'row')
The draws below stay inside these ranges and needn't reach their ends.
Inputs may be any that keep to these rules, and one draw needn't show every extreme that they name: `block_cols`: the 2 column blocks of one row block and group are different.
All inputs are finite; a program needn't handle non-finite values.
Results may differ from the reference program's by a relative error of at most 0.0071.
The reference program's roundings to bfloat16 on the way (of `cell`) count: a program that leaves them out, or rounds other values in their place, can miss the bound.
Values may be sent and summed in bfloat16 or wider, within the bound.
A program may use at most 128 MiB of HBM per device.

```python
import math
import jax
import jax.numpy as jnp
from jax import lax

D = 512
BLOCK = 1024
GROUP_BLOCKS = 4
SLOTS = 2
EXCLUDED = 512
ROW_BLOCKS = 64
GROUPS = 4
ROWS = 65536
GROUP_COLS = 4096


def draw_counts(key, part):
    shape = (ROW_BLOCKS, GROUPS, SLOTS, BLOCK, BLOCK)
    key_level = jax.random.fold_in(key, 11)
    key_value = jax.random.fold_in(key, 23)
    level = jax.random.randint(key_level, shape, -3, 11)
    ceiling = jnp.left_shift(jnp.int32(1), jnp.maximum(level, 0)) + 1
    value = jax.random.randint(key_value, shape, 1, ceiling)
    return jnp.where(level >= 0, value, 0).astype(jnp.int32)


def set_ends(result, rng, least, largest):
    longest = result.shape.index(max(result.shape))
    spots = []
    for shift in (0, 1):
        where = [jax.random.randint(jax.random.fold_in(rng, axis), (), 0, length) for axis, length in enumerate(result.shape)]
        where[longest] = (where[longest] + shift) % result.shape[longest]
        spots.append(tuple(where))
    return result.at[spots[0]].set(least).at[spots[1]].set(largest)


def block_levels(rng, shape, cuts, low, largest):
    loudness = 1.0
    for dim, blocks in cuts:
        heights = jax.random.uniform(jax.random.fold_in(jax.random.fold_in(rng, 6), dim), (blocks,), jnp.float32, low / len(cuts), largest / len(cuts))
        loudness = loudness * jnp.repeat(jnp.exp(heights), shape[dim] // blocks).reshape((-1,) + (1,) * (len(shape) - 1 - dim))
    return loudness


def different_ones(own_key, rows, amount, top, lift):
    sequence = jax.random.permutation(jax.random.fold_in(own_key, 1), amount)
    favour = sequence
    for power in range(3):
        favour = favour * favour // amount
    favour = favour * lift // amount
    chance = jax.random.randint(jax.random.fold_in(own_key, 2), (rows, amount), 0, 4096) + favour
    holders = jax.random.permutation(jax.random.fold_in(own_key, 3), rows)[jnp.arange(amount) % rows]
    chance = jnp.where(jnp.arange(rows)[:, None] == holders[None, :], 1 << 14, chance)
    score = chance * amount + jnp.arange(amount)
    return lax.top_k(score.astype(jnp.int32), top)[1].astype(jnp.int32)


def bell_draw(key, shape, scale, reach, cuts=(), held_as=jnp.bfloat16):
    drawn = scale * jax.random.normal(key, shape, jnp.float32)
    if cuts:
        drawn = drawn * block_levels(key, shape, cuts, -0.22, 0.18)
    return jnp.clip(drawn, -reach, reach).astype(held_as)


def setup_inputs(seed: int = 0) -> dict:
    key_of = jax.random.split(jax.random.key(seed), 11)
    return {
        "row_embed": bell_draw(key_of[0], (ROWS, D), 0.25, 1.5, ((0, 256),), jnp.float32),
        "row_accum": jnp.clip(jnp.exp(math.log(0.01) - 2.30258502 * jax.random.uniform(key_of[1], (ROWS, D), jnp.float32) ** block_levels(key_of[1], (ROWS, D), ((0, 256),), -0.2, 0.2)), 0.001, 0.01),
        "col_embed": bell_draw(key_of[2], (GROUPS, GROUP_COLS, D), 0.25, 1.5, ((0, 4), (1, 64)), jnp.float32),
        "col_accum": jnp.clip(jnp.exp(math.log(0.01) - 2.30258502 * jax.random.uniform(key_of[3], (GROUPS, GROUP_COLS, D), jnp.float32) ** block_levels(key_of[3], (GROUPS, GROUP_COLS, D), ((0, 4), (1, 64)), -0.2, 0.2)), 0.001, 0.01),
        "col_freq": set_ends(jax.random.randint(key_of[4], (GROUPS, GROUP_COLS), 1000, 30000), jax.random.fold_in(key_of[4], 1), 1000, 29999).astype(jnp.int32),
        "row_freq": set_ends(jax.random.randint(key_of[5], (ROWS,), 1000, 30000), jax.random.fold_in(key_of[5], 1), 1000, 29999).astype(jnp.int32),
        "block_cols": different_ones(key_of[6], ROW_BLOCKS * GROUPS, GROUP_BLOCKS, SLOTS, 4096).reshape((ROW_BLOCKS, GROUPS, SLOTS)),
        "counts": draw_counts(jax.random.fold_in(key_of[10], 71), 0),
        "excluded": set_ends(jax.random.randint(key_of[8], (EXCLUDED,), 0, ROWS), jax.random.fold_in(key_of[8], 1), 0, ROWS - 1).astype(jnp.int32),
        "log_total": jnp.clip(jax.random.uniform(key_of[9], (), jnp.float32, 15.0, 19.0), 15.0, 19.0),
    }


learn_rate = 0.2
decay_rate = 0.5

def cell_grads(count_block, predicted, row_logs, col_logs, log_total):
    nonzero = count_block > 0
    safe_count = jnp.where(nonzero, count_block.astype(jnp.float32), jnp.float32(1.0))
    baseline = log_total - row_logs[:, None] - col_logs[None, :]
    weight = 0.1 + 0.25 * jnp.sqrt(safe_count)
    fitted = weight * (predicted - baseline - jnp.log(safe_count))
    hinge_grad = jax.nn.sigmoid(predicted - baseline)
    return (jnp.where(nonzero, fitted, hinge_grad) / BLOCK).astype(jnp.bfloat16)

def reference(row_embed, row_accum, col_embed, col_accum, col_freq, row_freq, block_cols, counts, excluded, log_total):
    row_half = row_embed.astype(jnp.bfloat16)
    col_half = col_embed.astype(jnp.bfloat16)
    row_logs = jnp.log(row_freq.astype(jnp.float32))
    col_logs = jnp.log(col_freq.astype(jnp.float32))
    zero = jnp.int32(0)

    def one_block(step, gradients):
        row_grad, col_grad = gradients
        step = jnp.asarray(step).astype(jnp.int32)
        row_index = step // (GROUPS * SLOTS)
        group_index = step // SLOTS % GROUPS
        slot_index = step % SLOTS
        chosen = block_cols[row_index, group_index, slot_index].astype(jnp.int32)
        row_start = row_index * BLOCK
        col_start = chosen * BLOCK
        row_block = lax.dynamic_slice(row_half, (row_start, zero), (BLOCK, D))
        col_block = lax.dynamic_slice(col_half, (group_index, col_start, zero), (1, BLOCK, D))[0]
        block_row_logs = lax.dynamic_slice(row_logs, (row_start,), (BLOCK,))
        block_col_logs = lax.dynamic_slice(col_logs, (group_index, col_start), (1, BLOCK))[0]
        count_block = lax.dynamic_slice(counts, (row_index, group_index, slot_index, zero, zero), (1, 1, 1, BLOCK, BLOCK))[0, 0, 0]
        predicted = jnp.dot(row_block, col_block.T, preferred_element_type=jnp.float32)
        cell = cell_grads(count_block, predicted, block_row_logs, block_col_logs, log_total)
        row_part = jnp.dot(cell, col_block, preferred_element_type=jnp.float32)
        col_part = jnp.dot(cell.T, row_block, preferred_element_type=jnp.float32)
        old_rows = lax.dynamic_slice(row_grad, (row_start, zero), (BLOCK, D))
        row_grad = lax.dynamic_update_slice(row_grad, old_rows + row_part, (row_start, zero))
        old_cols = lax.dynamic_slice(col_grad, (group_index, col_start, zero), (1, BLOCK, D))
        col_grad = lax.dynamic_update_slice(col_grad, old_cols + col_part[None], (group_index, col_start, zero))
        return (row_grad, col_grad)
    start_rows = jnp.zeros((ROWS, D), jnp.float32)
    start_cols = jnp.zeros((GROUPS, GROUP_COLS, D), jnp.float32)
    row_grad, col_grad = lax.fori_loop(0, ROW_BLOCKS * GROUPS * SLOTS, one_block, (start_rows, start_cols))
    row_ids = jnp.arange(ROWS, dtype=jnp.int32)
    decayed = jnp.all(row_ids[:, None] != excluded[None, :], axis=1)
    freq_root = jnp.sqrt(row_freq.astype(jnp.float32))
    decay_coef = jnp.where(decayed, decay_rate * freq_root / (freq_root + 30.0), jnp.float32(0.0))
    full_grad = row_grad + decay_coef[:, None] * row_embed
    row_accum_new = row_accum + full_grad * full_grad
    row_embed_new = row_embed - learn_rate * full_grad / jnp.sqrt(row_accum_new)
    col_accum_new = col_accum + col_grad * col_grad
    col_embed_new = col_embed - learn_rate * col_grad / jnp.sqrt(col_accum_new)
    return (row_embed_new, row_accum_new, col_embed_new, col_accum_new)
```

```python
import jax
import jax.numpy as jnp
from jax import lax
from jax.experimental import pallas as pl
from jax.experimental.pallas import tpu as pltpu
from jax.sharding import PartitionSpec as P

MESH = pl.DeviceIdType.MESH
NX, NY, NZ, NK = 4, 4, 8, 2
BLOCK = 1024
HALF = 512
PIECE = 64
QUARTER = 256
D = 512
F32 = jnp.float32
BF16 = jnp.bfloat16

learn_rate = 0.2
decay_rate = 0.5

GATHER_ORDER = (0, 2, 6, 4, 1, 7, 3, 5)
REDUCE_ORDER = (4, 2, 6, 0, 3, 5, 1, 7)


def pick(index, values):
    result = jnp.int32(values[-1])
    for place in range(len(values) - 1):
        result = jnp.where(index == place, jnp.int32(values[place]), result)
    return result


def step_kernel(
    chosen, total, row_own, col_own, row_freq, col_freq, counts,
    own_grad, col_grad,
    cols, mine, rows, cnt, wgt, base, cells, row_logs,
    part, pair_in, send_half, recv_half, send_full, recv_full, send_z, recv_z,
    xsend_half, xrecv_half, xsend_full, xrecv_full,
    cnt_sem, ag_s, ag_r, rs_s, rs_r, x_s, x_r,
):
    r = lax.axis_index("row")
    x = lax.axis_index("col")
    k = lax.rem(r, NK)
    y = lax.rem(r // NK, NY)
    z = r // (NK * NY)
    yp, ym, y2 = lax.rem(y + 1, NY), lax.rem(y + 3, NY), lax.rem(y + 2, NY)
    xp, xm, x2 = lax.rem(x + 1, NX), lax.rem(x + 3, NX), lax.rem(x + 2, NX)
    other = 1 - k

    def dev(dx, dy, dz, dk):
        return ((dz * NY + dy) * NK + dk, dx)

    right, left = dev(x, yp, z, k), dev(x, ym, z, k)
    east, west = dev(xp, y, z, k), dev(xm, y, z, k)
    mate = dev(x, y, z, other)

    def remote(src, dst, s, q, target):
        return pltpu.make_async_remote_copy(
            src_ref=src, dst_ref=dst, send_sem=s, recv_sem=q, device_id=target, device_id_type=MESH
        )

    def count_copy(c):
        h, s, b = c // 4, (c // 2) % 2, c % 2
        lane = pl.multiple_of(lax.rem(z + h, 2) * HALF, HALF)
        return pltpu.make_async_copy(
            counts.at[s, pl.ds(b * HALF, HALF), pl.ds(lane, HALF)],
            cnt.at[s, h, pl.ds(b * HALF, HALF)],
            cnt_sem.at[c],
        )

    for c in range(8):
        count_copy(c).start()

    barrier = pltpu.get_barrier_semaphore()
    for target in (right, left, east, west, mate):
        pl.semaphore_signal(barrier, inc=1, device_id=target, device_id_type=MESH)
    for dz in range(1, NZ):
        pl.semaphore_signal(
            barrier, inc=1, device_id=dev(x, y, lax.rem(z + dz, NZ), k), device_id_type=MESH
        )
    cols[z, y, k] = col_own[...].astype(BF16)
    my_rows = pl.multiple_of(x * QUARTER, QUARTER)
    rows[pl.ds(my_rows, QUARTER)] = row_own[...].astype(BF16)
    pl.semaphore_wait(barrier, 5 + NZ - 1)

    def z_copy(i):
        zt = lax.rem(z + GATHER_ORDER[i], NZ)
        return remote(cols.at[z, y, k], cols.at[z, y, k], ag_s.at[0, i], ag_r.at[0, z], dev(x, y, zt, k))

    def z_arrival(zs):
        return remote(cols.at[zs, y, k], cols.at[zs, y, k], ag_s.at[0, 0], ag_r.at[0, zs], mate)

    def y_copy(zs, up):
        kind, target = (1, right) if up else (2, left)
        return remote(cols.at[zs, y, k], cols.at[zs, y, k], ag_s.at[kind, zs], ag_r.at[kind, zs], target)

    def y_arrival(zs, up):
        kind, src = (1, ym) if up else (2, yp)
        return remote(cols.at[zs, src, k], cols.at[zs, src, k], ag_s.at[kind, zs], ag_r.at[kind, zs], mate)

    def y_forward(zs, up):
        kind, src, start, target = (3, ym, 0, right) if up else (4, yp, PIECE // 2, left)
        ref = cols.at[zs, src, k, pl.ds(start, PIECE // 2)]
        return remote(ref, ref, ag_s.at[kind, zs], ag_r.at[kind, zs], target)

    def y_far(zs, up):
        kind, start = (3, 0) if up else (4, PIECE // 2)
        ref = cols.at[zs, y2, k, pl.ds(start, PIECE // 2)]
        return remote(ref, ref, ag_s.at[kind, zs], ag_r.at[kind, zs], mate)

    def mate_copy(zs):
        return remote(cols.at[zs, :, k], cols.at[zs, :, k], ag_s.at[5, zs], ag_r.at[5, zs], mate)

    def mate_arrival(zs):
        return remote(cols.at[zs, :, other], cols.at[zs, :, other], ag_s.at[5, zs], ag_r.at[5, zs], mate)

    def quarter(q, start, size):
        return rows.at[pl.ds(pl.multiple_of(q * QUARTER + start, 128), size)]

    def x_copy(i):
        n = 128
        q, start, target = ((x, 0, east), (x, n, west), (x, n, east), (x, 0, west), (xm, 0, east), (xp, n, west))[i]
        return remote(quarter(q, start, n), quarter(q, start, n), x_s.at[i], x_r.at[i], target)

    def x_arrival(i):
        n = 128
        q, start = ((xm, 0), (xp, n), (xm, n), (xp, 0), (x2, 0), (x2, n))[i]
        return remote(quarter(q, start, n), quarter(q, start, n), x_s.at[i], x_r.at[i], mate)

    y_copy(z, True).start()
    y_copy(z, False).start()
    for i in range(1, NZ):
        z_copy(i).start()
    for i in range(4):
        x_copy(i).start()

    logs = jnp.log(row_freq[...].astype(F32)) - total[0]
    row_logs[...] = jnp.broadcast_to(logs, (128, BLOCK)).T

    def of_block(block, options):
        result = options[3]
        for b in range(3):
            result = lax.select(block == b, options[b], result)
        return result

    def prepare(c):
        h, s = c // 4, lax.rem(c // 2, 2)
        first = lax.rem(c, 2) * HALF
        ref = cnt.at[s, h, pl.ds(first, HALF)]
        pltpu.make_async_copy(ref, ref, cnt_sem.at[c]).wait()
        parity = lax.rem(z + h, 2)
        freq = of_block(
            chosen[s],
            [col_freq[:, pl.ds(pl.multiple_of(b * BLOCK + parity * HALF, HALF), HALF)] for b in range(4)],
        )
        col_logs = jnp.log(freq.astype(F32))

        def tile(n, _):
            at = pl.ds(pl.multiple_of(first + n * PIECE, PIECE), PIECE)
            rl = row_logs[at]
            for lane in range(0, HALF, 128):
                count = cnt[s, h, at, lane : lane + 128]
                full = count > 0
                value = jnp.maximum(count, 1).astype(F32)
                root = value * lax.rsqrt(value)
                base[s, h, at, lane : lane + 128] = (rl + col_logs[:, lane : lane + 128]) - jnp.log(value)
                wgt[s, h, at, lane : lane + 128] = jnp.where(
                    full, (0.1 / BLOCK) + (0.25 / BLOCK) * root, 0.0
                )
            return 0

        lax.fori_loop(0, HALF // PIECE, tile, 0)

    def cell_tile(h, n):
        s, q = n // 2, lax.rem(n, 2)
        parity = lax.rem(z + h, 2)
        col_tile = of_block(
            chosen[s], [cols[2 * b + parity, pl.ds(2 * q, 2)].reshape(QUARTER, D) for b in range(4)]
        )
        mine[s, h, q] = col_tile
        lane = pl.multiple_of(q * QUARTER, QUARTER)
        for m in range(4):
            at = pl.ds(m * QUARTER, QUARTER)
            predicted = lax.dot_general(
                rows[at], col_tile, (((1,), (1,)), ((), ())), preferred_element_type=F32
            )
            shifted = predicted + base[s, h, at, pl.ds(lane, QUARTER)]
            w = wgt[s, h, at, pl.ds(lane, QUARTER)]
            hinge = 1.0 / (BLOCK + BLOCK * jnp.exp(-shifted))
            cells[s, h, at, pl.ds(lane, QUARTER)] = jnp.where(w > 0.0, w * shifted, hinge).astype(BF16)

    def gather_step(i, _):
        @pl.when(i < 8)
        def _():
            zs = lax.rem(z + pick(i, GATHER_ORDER), NZ)

            @pl.when(i > 0)
            def _():
                z_arrival(zs).wait_recv()
                y_copy(zs, True).start()
                y_copy(zs, False).start()

        @pl.when((i >= 1) & (i < 9))
        def _():
            zs = lax.rem(z + pick(i - 1, GATHER_ORDER), NZ)
            y_arrival(zs, True).wait_recv()
            y_forward(zs, True).start()
            y_arrival(zs, False).wait_recv()
            y_forward(zs, False).start()

        @pl.when((i >= 2) & (i < 10))
        def _():
            zs = lax.rem(z + pick(i - 2, GATHER_ORDER), NZ)
            y_far(zs, True).wait_recv()
            y_far(zs, False).wait_recv()
            mate_copy(zs).start()

        @pl.when(i == 2)
        def _():
            for j in range(2):
                x_arrival(j).wait_recv()
                x_copy(4 + j).start()

        @pl.when(i < 4)
        def _():
            prepare(2 * i)
            prepare(2 * i + 1)

        @pl.when(i == 6)
        def _():
            for j in range(2, 6):
                x_arrival(j).wait_recv()
            for j in range(4):
                mate_arrival(lax.rem(z + GATHER_ORDER[j], NZ)).wait_recv()

        @pl.when(i >= 6)
        def _():
            cell_tile(0, i - 6)

        return 0

    lax.fori_loop(0, 10, gather_step, 0)
    for j in range(4, 8):
        mate_arrival(lax.rem(z + GATHER_ORDER[j], NZ)).wait_recv()

    def mate_send(i):
        return remote(part.at[i, :, other], pair_in.at[i], rs_s.at[0, i], rs_r.at[0, i], mate)

    def mate_recv(i):
        return remote(pair_in.at[i], pair_in.at[i], rs_s.at[0, i], rs_r.at[0, i], mate)

    def half_copy(i, up):
        n, target = (0, right) if up else (1, left)
        return remote(send_half.at[n, i], recv_half.at[n, i], rs_s.at[1 + n, i], rs_r.at[1 + n, i], target)

    def full_copy(i, up):
        n, target = (0, right) if up else (1, left)
        return remote(send_full.at[n, i], recv_full.at[n, i], rs_s.at[3 + n, i], rs_r.at[3 + n, i], target)

    def home_copy(i):
        zt = lax.rem(z + pick(i, REDUCE_ORDER), NZ)
        return remote(send_z.at[i], recv_z.at[i], rs_s.at[5, i], rs_r.at[5, i], dev(x, y, zt, k))

    def chip_sum(i, dest):
        return part[i, dest, k] + pair_in[i, dest]

    def col_part(i):
        shift = pick(i, REDUCE_ORDER)
        zt = lax.rem(z + shift, NZ)
        h = lax.rem(shift, 2)
        b = zt // 2
        for q in range(2):
            lanes = slice(q * QUARTER, (q + 1) * QUARTER)
            cell = lax.select(chosen[1] == b, cells[1, h, :, lanes], jnp.zeros((BLOCK, QUARTER), BF16))
            found = lax.dot_general(
                lax.select(chosen[0] == b, cells[0, h, :, lanes], cell),
                rows[...],
                (((0,), (0,)), ((), ())),
                preferred_element_type=F32,
            )
            part[i, 2 * q : 2 * q + 2] = found.reshape(2, NK, PIECE, D)

    def row_part(q):
        at = pl.ds(pl.multiple_of(q * QUARTER, QUARTER), QUARTER)
        result = jnp.zeros((QUARTER, D), F32)
        for s in range(2):
            for h in range(2):
                result = result + jnp.dot(
                    cells[s, h, at], mine[s, h].reshape(HALF, D), preferred_element_type=F32
                )
        return result

    def xhalf(up):
        n, target = (0, east) if up else (1, west)
        return remote(xsend_half.at[n], xrecv_half.at[n], x_s.at[6 + n], x_r.at[6 + n], target)

    def xfull(up):
        n, target = (0, east) if up else (1, west)
        return remote(xsend_full.at[n], xrecv_full.at[n], x_s.at[8 + n], x_r.at[8 + n], target)

    lower = PIECE // 2

    def reduce_step(i, _):
        @pl.when((i >= 1) & (i < 9))
        def _():
            j = i - 1
            mate_recv(j).wait_recv()
            value = chip_sum(j, y2).astype(BF16)
            send_half[0, j] = value[:lower]
            half_copy(j, True).start()
            send_half[1, j] = value[lower:]
            half_copy(j, False).start()

        @pl.when((i >= 2) & (i < 10))
        def _():
            j = i - 2
            half_copy(j, True).wait_recv()
            value = chip_sum(j, yp)
            send_full[0, j, :lower] = (value[:lower] + recv_half[0, j].astype(F32)).astype(BF16)
            send_full[0, j, lower:] = value[lower:].astype(BF16)
            full_copy(j, True).start()
            half_copy(j, False).wait_recv()
            value = chip_sum(j, ym)
            send_full[1, j, :lower] = value[:lower].astype(BF16)
            send_full[1, j, lower:] = (value[lower:] + recv_half[1, j].astype(F32)).astype(BF16)
            full_copy(j, False).start()

        @pl.when(i >= 3)
        def _():
            j = i - 3
            full_copy(j, True).wait_recv()
            full_copy(j, False).wait_recv()
            value = chip_sum(j, y) + recv_full[0, j].astype(F32) + recv_full[1, j].astype(F32)

            @pl.when(j == 3)
            def _():
                col_grad[...] = value

            @pl.when(j != 3)
            def _():
                send_z[j] = value.astype(BF16)
                home_copy(j).start()

        @pl.when(i < 4)
        def _():
            cell_tile(1, i)

        @pl.when(i < 8)
        def _():
            col_part(i)
            mate_send(i).start()

        @pl.when(i == 4)
        def _():
            value = row_part(x2).astype(BF16)
            xsend_half[0] = value[:128]
            xsend_half[1] = value[128:]
            xhalf(True).start()
            xhalf(False).start()

        @pl.when(i == 5)
        def _():
            value = row_part(xp)
            xhalf(True).wait_recv()
            xsend_full[0, :128] = (value[:128] + xrecv_half[0].astype(F32)).astype(BF16)
            xsend_full[0, 128:] = value[128:].astype(BF16)
            xfull(True).start()

        @pl.when(i == 6)
        def _():
            value = row_part(xm)
            xhalf(False).wait_recv()
            xsend_full[1, :128] = value[:128].astype(BF16)
            xsend_full[1, 128:] = (value[128:] + xrecv_half[1].astype(F32)).astype(BF16)
            xfull(False).start()

        @pl.when(i == 7)
        def _():
            own_grad[...] = row_part(x)

        return 0

    lax.fori_loop(0, 11, reduce_step, 0)
    xfull(True).wait_recv()
    xfull(False).wait_recv()
    own_grad[...] += xrecv_full[0].astype(F32) + xrecv_full[1].astype(F32)
    for j in (0, 1, 2, 4, 5, 6, 7):
        home_copy(j).wait_recv()
        col_grad[...] += recv_z[j].astype(F32)

    for j in range(1, NZ):
        z_copy(j).wait_send()

    def drain(j, _):
        for up in (True, False):
            y_copy(j, up).wait_send()
            y_forward(j, up).wait_send()
            half_copy(j, up).wait_send()
            full_copy(j, up).wait_send()
        mate_copy(j).wait_send()
        mate_send(j).wait_send()

        @pl.when(j != 3)
        def _():
            home_copy(j).wait_send()

        return 0

    lax.fori_loop(0, NZ, drain, 0)
    for j in range(6):
        x_copy(j).wait_send()
    for up in (True, False):
        xhalf(up).wait_send()
        xfull(up).wait_send()


def gradients(row_embed, col_embed, row_freq, col_freq, block_cols, counts, log_total):
    vmem = pl.BlockSpec(memory_space=pltpu.VMEM)
    smem = pl.BlockSpec(memory_space=pltpu.SMEM)
    return pl.pallas_call(
        step_kernel,
        out_shape=(
            jax.ShapeDtypeStruct((QUARTER, D), F32),
            jax.ShapeDtypeStruct((PIECE, D), F32),
        ),
        in_specs=[smem, smem, vmem, vmem, vmem, vmem, pl.BlockSpec(memory_space=pl.ANY)],
        out_specs=(vmem, vmem),
        scratch_shapes=[
            pltpu.VMEM((NZ, NY, NK, PIECE, D), BF16),
            pltpu.VMEM((2, 2, 2, QUARTER, D), BF16),
            pltpu.VMEM((BLOCK, D), BF16),
            pltpu.VMEM((2, 2, BLOCK, HALF), jnp.int32),
            pltpu.VMEM((2, 2, BLOCK, HALF), F32),
            pltpu.VMEM((2, 2, BLOCK, HALF), F32),
            pltpu.VMEM((2, 2, BLOCK, HALF), BF16),
            pltpu.VMEM((BLOCK, 128), F32),
            pltpu.VMEM((NZ, NY, NK, PIECE, D), F32),
            pltpu.VMEM((NZ, NY, PIECE, D), F32),
            pltpu.VMEM((2, NZ, PIECE // 2, D), BF16),
            pltpu.VMEM((2, NZ, PIECE // 2, D), BF16),
            pltpu.VMEM((2, NZ, PIECE, D), BF16),
            pltpu.VMEM((2, NZ, PIECE, D), BF16),
            pltpu.VMEM((NZ, PIECE, D), BF16),
            pltpu.VMEM((NZ, PIECE, D), BF16),
            pltpu.VMEM((2, 128, D), BF16),
            pltpu.VMEM((2, 128, D), BF16),
            pltpu.VMEM((2, QUARTER, D), BF16),
            pltpu.VMEM((2, QUARTER, D), BF16),
            pltpu.SemaphoreType.DMA((8,)),
            pltpu.SemaphoreType.DMA((6, NZ)),
            pltpu.SemaphoreType.DMA((6, NZ)),
            pltpu.SemaphoreType.DMA((6, NZ)),
            pltpu.SemaphoreType.DMA((6, NZ)),
            pltpu.SemaphoreType.DMA((10,)),
            pltpu.SemaphoreType.DMA((10,)),
        ],
        compiler_params=pltpu.CompilerParams(
            collective_id=0, has_side_effects=True, vmem_limit_bytes=58 << 20
        ),
        cost_estimate=pl.CostEstimate(
            flops=8 << 30, bytes_accessed=12 << 20, transcendentals=8 << 20
        ),
        name="swivel_step",
    )(
        block_cols.reshape(2),
        log_total.reshape(1),
        row_embed,
        col_embed[0],
        row_freq.reshape(1, BLOCK),
        col_freq,
        counts[0, 0],
    )


def body(
    row_embed,
    row_accum,
    col_embed,
    col_accum,
    col_freq,
    row_freq,
    block_cols,
    counts,
    excluded,
    log_total,
):
    own_rows = row_embed.shape[0]
    col_index = lax.axis_index("col")
    row_index = lax.axis_index("row")
    own_freq = lax.dynamic_slice_in_dim(row_freq, col_index * own_rows, own_rows).astype(F32)
    row_ids = row_index * BLOCK + col_index * own_rows + jnp.arange(own_rows, dtype=jnp.int32)
    decayed = jnp.all(row_ids[:, None] != excluded[None, :], axis=1)
    freq_root = jnp.sqrt(own_freq)
    decay_coef = jnp.where(decayed, decay_rate * freq_root / (freq_root + 30.0), F32(0.0))
    own_grad, col_grad = gradients(
        row_embed, col_embed, row_freq, col_freq, block_cols, counts, log_total
    )
    full_grad = own_grad + decay_coef[:, None] * row_embed
    row_accum_new = row_accum + full_grad * full_grad
    row_embed_new = row_embed - learn_rate * full_grad / jnp.sqrt(row_accum_new)
    col_step = col_grad[None]
    col_accum_new = col_accum + col_step * col_step
    col_embed_new = col_embed - learn_rate * col_step / jnp.sqrt(col_accum_new)
    return (row_embed_new, row_accum_new, col_embed_new, col_accum_new)


def solution(mesh):
    in_specs = (
        P(("row", "col"), None),
        P(("row", "col"), None),
        P("col", "row", None),
        P("col", "row", None),
        P("col", None),
        P("row"),
        P("row", "col", None),
        P("row", "col", None, None, None),
        P(),
        P(),
    )
    out_specs = (
        P(("row", "col"), None),
        P(("row", "col"), None),
        P("col", "row", None),
        P("col", "row", None),
    )
    return jax.shard_map(body, mesh=mesh, in_specs=in_specs, out_specs=out_specs, check_vma=False)
```

```python
import jax
import jax.numpy as jnp
from jax import lax
from jax.experimental import pallas as pl
from jax.experimental.pallas import tpu as pltpu
from jax.sharding import PartitionSpec as P

MESH = pl.DeviceIdType.MESH
NX, NY, NZ, NK = 4, 4, 8, 2
BLOCK = 1024
HALF = 512
EXCLUDED = 512
PIECE = 64
QUARTER = 256
D = 512
F32 = jnp.float32
BF16 = jnp.bfloat16

learn_rate = 0.2
decay_rate = 0.5

GATHER_ORDER = (0, 2, 6, 4, 1, 7, 3, 5)
REDUCE_ORDER = (4, 2, 6, 0, 3, 5, 1, 7)

GATHER_MORE = 1
GATHER_NEAR = 2
GATHER_FAR = 4
CELLS = 8
REDUCE = 10
CELLS_MORE = REDUCE + 2
REDUCE_FAR = REDUCE + 2
REDUCE_NEAR = REDUCE + 4
REDUCE_HOME = REDUCE + 6
ROWS = REDUCE + 5


def pick(index, values):
    result = jnp.int32(values[-1])
    for place in range(len(values) - 1):
        result = jnp.where(index == place, jnp.int32(values[place]), result)
    return result


def step_kernel(
    chosen, total, row_local, col_local, row_freq, col_freq, excluded, row_accum, col_accum, counts,
    result,
    made, own_grad, col_grad, row_sums, col_sums, decay,
    cols, mine, rows, cnt, wgt, base, cells, row_logs,
    part, pair_in, send_half, recv_half, send_full, recv_full, send_z, recv_z,
    xsend_half, xrecv_half, xsend_full, xrecv_full,
    cnt_sem, ag_s, ag_r, rs_s, rs_r, x_s, x_r,
):
    r = lax.axis_index("row")
    x = lax.axis_index("col")
    k = lax.rem(r, NK)
    y = lax.rem(r // NK, NY)
    z = r // (NK * NY)
    yp, ym, y2 = lax.rem(y + 1, NY), lax.rem(y + 3, NY), lax.rem(y + 2, NY)
    xp, xm, x2 = lax.rem(x + 1, NX), lax.rem(x + 3, NX), lax.rem(x + 2, NX)
    other = 1 - k

    def dev(dx, dy, dz, dk):
        return ((dz * NY + dy) * NK + dk, dx)

    right, left = dev(x, yp, z, k), dev(x, ym, z, k)
    east, west = dev(xp, y, z, k), dev(xm, y, z, k)
    mate = dev(x, y, z, other)

    def remote(src, dst, s, q, target):
        return pltpu.make_async_remote_copy(
            src_ref=src, dst_ref=dst, send_sem=s, recv_sem=q, device_id=target, device_id_type=MESH
        )

    def count_copy(c):
        h, s, b = c // 4, (c // 2) % 2, c % 2
        lane = pl.multiple_of(lax.rem(z + h, 2) * HALF, HALF)
        return pltpu.make_async_copy(
            counts.at[s, pl.ds(b * HALF, HALF), pl.ds(lane, HALF)],
            cnt.at[s, h, pl.ds(b * HALF, HALF)],
            cnt_sem.at[c],
        )

    def sums_copy(i):
        return pltpu.make_async_copy(
            (row_accum, col_accum)[i], (row_sums, col_sums)[i], cnt_sem.at[8 + i]
        )

    for c in range(8):
        count_copy(c).start()
    for i in range(2):
        sums_copy(i).start()

    barrier = pltpu.get_barrier_semaphore()
    for target in (right, left, east, west, mate):
        pl.semaphore_signal(barrier, inc=1, device_id=target, device_id_type=MESH)
    for dz in range(1, NZ):
        pl.semaphore_signal(
            barrier, inc=1, device_id=dev(x, y, lax.rem(z + dz, NZ), k), device_id_type=MESH
        )
    cols[z, y, k] = col_local[...].astype(BF16)
    my_rows = pl.multiple_of(x * QUARTER, QUARTER)
    rows[pl.ds(my_rows, QUARTER)] = row_local[...].astype(BF16)
    pl.semaphore_wait(barrier, 5 + NZ - 1)

    def z_copy(i):
        zt = lax.rem(z + pick(i, GATHER_ORDER), NZ)
        return remote(cols.at[z, y, k], cols.at[z, y, k], ag_s.at[0, i], ag_r.at[0, z], dev(x, y, zt, k))

    def z_arrival(zs):
        return remote(cols.at[zs, y, k], cols.at[zs, y, k], ag_s.at[0, 0], ag_r.at[0, zs], mate)

    def y_copy(zs, up):
        kind, target = (1, right) if up else (2, left)
        return remote(cols.at[zs, y, k], cols.at[zs, y, k], ag_s.at[kind, zs], ag_r.at[kind, zs], target)

    def y_arrival(zs, up):
        kind, src = (1, ym) if up else (2, yp)
        return remote(cols.at[zs, src, k], cols.at[zs, src, k], ag_s.at[kind, zs], ag_r.at[kind, zs], mate)

    def y_forward(zs, up):
        kind, src, start, target = (3, ym, 0, right) if up else (4, yp, PIECE // 2, left)
        ref = cols.at[zs, src, k, pl.ds(start, PIECE // 2)]
        return remote(ref, ref, ag_s.at[kind, zs], ag_r.at[kind, zs], target)

    def y_far(zs, up):
        kind, start = (3, 0) if up else (4, PIECE // 2)
        ref = cols.at[zs, y2, k, pl.ds(start, PIECE // 2)]
        return remote(ref, ref, ag_s.at[kind, zs], ag_r.at[kind, zs], mate)

    def mate_copy(zs):
        return remote(cols.at[zs, :, k], cols.at[zs, :, k], ag_s.at[5, zs], ag_r.at[5, zs], mate)

    def mate_arrival(zs):
        return remote(cols.at[zs, :, other], cols.at[zs, :, other], ag_s.at[5, zs], ag_r.at[5, zs], mate)

    def quarter(q, start, size):
        return rows.at[pl.ds(pl.multiple_of(q * QUARTER + start, 128), size)]

    def x_copy(i):
        n = 128
        q, start, target = ((x, 0, east), (x, n, west), (x, n, east), (x, 0, west), (xm, 0, east), (xp, n, west))[i]
        return remote(quarter(q, start, n), quarter(q, start, n), x_s.at[i], x_r.at[i], target)

    def x_arrival(i):
        n = 128
        q, start = ((xm, 0), (xp, n), (xm, n), (xp, 0), (x2, 0), (x2, n))[i]
        return remote(quarter(q, start, n), quarter(q, start, n), x_s.at[i], x_r.at[i], mate)

    y_copy(z, True).start()
    y_copy(z, False).start()
    for i in range(1, 4):
        z_copy(i).start()
    for i in range(4):
        x_copy(i).start()

    logs = jnp.log(row_freq[...].astype(F32)) - total[0]
    row_logs[...] = jnp.broadcast_to(logs, (128, BLOCK)).T

    ids = r * BLOCK + my_rows + lax.broadcasted_iota(jnp.int32, (QUARTER, EXCLUDED), 0)
    listed = jnp.max(jnp.where(ids == excluded[...], 1.0, 0.0), axis=1, keepdims=True)
    root = jnp.sqrt(row_freq[:, pl.ds(my_rows, QUARTER)].astype(F32))
    coef = jnp.broadcast_to(decay_rate * root / (root + 30.0), (128, QUARTER)).T
    decay[...] = jnp.where(listed > 0.0, 0.0, coef)

    def of_block(block, options):
        result = options[3]
        for b in range(3):
            result = lax.select(block == b, options[b], result)
        return result

    def prepare(c):
        h, s = c // 4, lax.rem(c // 2, 2)
        first = lax.rem(c, 2) * HALF
        ref = cnt.at[s, h, pl.ds(first, HALF)]
        pltpu.make_async_copy(ref, ref, cnt_sem.at[c]).wait()
        parity = lax.rem(z + h, 2)
        freq = of_block(
            chosen[s],
            [col_freq[:, pl.ds(pl.multiple_of(b * BLOCK + parity * HALF, HALF), HALF)] for b in range(4)],
        )
        col_logs = jnp.log(freq.astype(F32))

        def tile(n, _):
            at = pl.ds(pl.multiple_of(first + n * PIECE, PIECE), PIECE)
            rl = row_logs[at]
            for lane in range(0, HALF, 128):
                count = cnt[s, h, at, lane : lane + 128]
                full = count > 0
                value = jnp.maximum(count, 1).astype(F32)
                root = value * lax.rsqrt(value)
                base[s, h, at, lane : lane + 128] = (rl + col_logs[:, lane : lane + 128]) - jnp.log(value)
                wgt[s, h, at, lane : lane + 128] = jnp.where(
                    full, (0.1 / BLOCK) + (0.25 / BLOCK) * root, 0.0
                )
            return 0

        lax.fori_loop(0, HALF // PIECE, tile, 0)

    def cell_tile(h, n):
        s, q = n // 2, lax.rem(n, 2)
        parity = lax.rem(z + h, 2)
        col_tile = of_block(
            chosen[s], [cols[2 * b + parity, pl.ds(2 * q, 2)].reshape(QUARTER, D) for b in range(4)]
        )
        mine[s, h, q] = col_tile
        lane = pl.multiple_of(q * QUARTER, QUARTER)
        for m in range(4):
            at = pl.ds(m * QUARTER, QUARTER)
            predicted = lax.dot_general(
                rows[at], col_tile, (((1,), (1,)), ((), ())), preferred_element_type=F32
            )
            shifted = predicted + base[s, h, at, pl.ds(lane, QUARTER)]
            w = wgt[s, h, at, pl.ds(lane, QUARTER)]
            hinge = 1.0 / (BLOCK + BLOCK * jnp.exp(-shifted))
            cells[s, h, at, pl.ds(lane, QUARTER)] = jnp.where(w > 0.0, w * shifted, hinge).astype(BF16)

    def mate_send(i):
        return remote(part.at[i, :, other], pair_in.at[i], rs_s.at[0, i], rs_r.at[0, i], mate)

    def mate_recv(i):
        return remote(pair_in.at[i], pair_in.at[i], rs_s.at[0, i], rs_r.at[0, i], mate)

    def half_copy(i, up):
        n, target = (0, right) if up else (1, left)
        return remote(send_half.at[n, i], recv_half.at[n, i], rs_s.at[1 + n, i], rs_r.at[1 + n, i], target)

    def full_copy(i, up):
        n, target = (0, right) if up else (1, left)
        return remote(send_full.at[n, i], recv_full.at[n, i], rs_s.at[3 + n, i], rs_r.at[3 + n, i], target)

    def home_copy(i):
        zt = lax.rem(z + pick(i, REDUCE_ORDER), NZ)
        return remote(send_z.at[i], recv_z.at[i], rs_s.at[5, i], rs_r.at[5, i], dev(x, y, zt, k))

    def chip_sum(i, dest):
        return part[i, dest, k] + pair_in[i, dest]

    def col_part(i):
        shift = pick(i, REDUCE_ORDER)
        zt = lax.rem(z + shift, NZ)
        h = lax.rem(shift, 2)
        b = zt // 2
        for q in range(2):
            lanes = slice(q * QUARTER, (q + 1) * QUARTER)
            cell = lax.select(chosen[1] == b, cells[1, h, :, lanes], jnp.zeros((BLOCK, QUARTER), BF16))
            found = lax.dot_general(
                lax.select(chosen[0] == b, cells[0, h, :, lanes], cell),
                rows[...],
                (((0,), (0,)), ((), ())),
                preferred_element_type=F32,
            )
            part[i, 2 * q : 2 * q + 2] = found.reshape(2, NK, PIECE, D)

    def row_part(q):
        at = pl.ds(pl.multiple_of(q * QUARTER, QUARTER), QUARTER)
        result = jnp.zeros((QUARTER, D), F32)
        for s in range(2):
            for h in range(2):
                result = result + jnp.dot(
                    cells[s, h, at], mine[s, h].reshape(HALF, D), preferred_element_type=F32
                )
        return result

    def xhalf(up):
        n, target = (0, east) if up else (1, west)
        return remote(xsend_half.at[n], xrecv_half.at[n], x_s.at[6 + n], x_r.at[6 + n], target)

    def xfull(up):
        n, target = (0, east) if up else (1, west)
        return remote(xsend_full.at[n], xrecv_full.at[n], x_s.at[8 + n], x_r.at[8 + n], target)

    lower = PIECE // 2

    def at_step(t, first, count, work):
        @pl.when((t >= first) & (t < first + count))
        def _():
            work(t - first)

    def gather_z(i):
        zs = lax.rem(z + pick(i, GATHER_ORDER), NZ)

        @pl.when(i > 0)
        def _():
            z_arrival(zs).wait_recv()
            y_copy(zs, True).start()
            y_copy(zs, False).start()

    def gather_more(i):
        z_copy(4 + i).start()

    def gather_near(i):
        zs = lax.rem(z + pick(i, GATHER_ORDER), NZ)
        y_arrival(zs, True).wait_recv()
        y_forward(zs, True).start()
        y_arrival(zs, False).wait_recv()
        y_forward(zs, False).start()

    def gather_far(i):
        zs = lax.rem(z + pick(i, GATHER_ORDER), NZ)
        y_far(zs, True).wait_recv()
        y_far(zs, False).wait_recv()
        mate_copy(zs).start()

    def gather_rows(_):
        for j in range(2):
            x_arrival(j).wait_recv()
            x_copy(4 + j).start()

    def half_ready(h):
        for j in range(4):
            mate_arrival(lax.rem(z + GATHER_ORDER[4 * h + j], NZ)).wait_recv()

    def rows_ready(_):
        for j in range(2, 6):
            x_arrival(j).wait_recv()

    def prepare_two(i):
        prepare(2 * i)
        prepare(2 * i + 1)

    def two_tiles(h, n):
        cell_tile(h, 2 * n)
        cell_tile(h, 2 * n + 1)

    def reduce_start(i):
        col_part(i)
        mate_send(i).start()

    def reduce_far(j):
        mate_recv(j).wait_recv()
        value = chip_sum(j, y2).astype(BF16)
        send_half[0, j] = value[:lower]
        half_copy(j, True).start()
        send_half[1, j] = value[lower:]
        half_copy(j, False).start()

    def reduce_near(j):
        half_copy(j, True).wait_recv()
        value = chip_sum(j, yp)
        send_full[0, j, :lower] = (value[:lower] + recv_half[0, j].astype(F32)).astype(BF16)
        send_full[0, j, lower:] = value[lower:].astype(BF16)
        full_copy(j, True).start()
        half_copy(j, False).wait_recv()
        value = chip_sum(j, ym)
        send_full[1, j, :lower] = value[:lower].astype(BF16)
        send_full[1, j, lower:] = (value[lower:] + recv_half[1, j].astype(F32)).astype(BF16)
        full_copy(j, False).start()

    def reduce_home(j):
        full_copy(j, True).wait_recv()
        full_copy(j, False).wait_recv()
        value = chip_sum(j, y) + recv_full[0, j].astype(F32) + recv_full[1, j].astype(F32)

        @pl.when(j == 3)
        def _():
            col_grad[...] = value

        @pl.when(j != 3)
        def _():
            send_z[j] = value.astype(BF16)
            home_copy(j).start()

    def row_far(_):
        value = row_part(x2).astype(BF16)
        xsend_half[0] = value[:128]
        xsend_half[1] = value[128:]
        xhalf(True).start()
        xhalf(False).start()

    def row_east(_):
        value = row_part(xp)
        xhalf(True).wait_recv()
        xsend_full[0, :128] = (value[:128] + xrecv_half[0].astype(F32)).astype(BF16)
        xsend_full[0, 128:] = value[128:].astype(BF16)
        xfull(True).start()

    def row_west(_):
        value = row_part(xm)
        xhalf(False).wait_recv()
        xsend_full[1, :128] = value[:128].astype(BF16)
        xsend_full[1, 128:] = (value[128:] + xrecv_half[1].astype(F32)).astype(BF16)
        xfull(False).start()

    def row_own(_):
        own_grad[...] = row_part(x)

    def result_copy(i):
        at = pl.ds((0, 2 * QUARTER)[i], (2 * QUARTER, 2 * PIECE)[i])
        return pltpu.make_async_copy(made.at[at], result.at[at], cnt_sem.at[10 + i])

    def row_update(_):
        sums_copy(0).wait()
        xfull(True).wait_recv()
        xfull(False).wait_recv()
        for lane in range(0, D, 128):
            at = slice(lane, lane + 128)
            value = row_local[:, at]
            grad = own_grad[:, at] + xrecv_full[0, :, at].astype(F32) + xrecv_full[1, :, at].astype(F32)
            grad = grad + decay[...] * value
            sums = row_sums[:, at] + grad * grad
            made[:QUARTER, at] = value - learn_rate * grad * lax.rsqrt(sums)
            made[QUARTER : 2 * QUARTER, at] = sums
        result_copy(0).start()

    def step(t, _):
        at_step(t, 0, 8, gather_z)
        at_step(t, GATHER_MORE, 4, gather_more)
        at_step(t, GATHER_NEAR, 8, gather_near)
        at_step(t, GATHER_FAR, 8, gather_far)
        at_step(t, 2, 1, gather_rows)
        at_step(t, REDUCE_HOME, 8, reduce_home)
        at_step(t, REDUCE_NEAR, 8, reduce_near)
        at_step(t, REDUCE_FAR, 8, reduce_far)
        at_step(t, 0, 4, prepare_two)
        at_step(t, CELLS, 1, rows_ready)
        at_step(t, CELLS, 1, lambda _: half_ready(0))
        at_step(t, CELLS, 2, lambda n: two_tiles(0, n))
        at_step(t, CELLS_MORE, 1, lambda _: half_ready(1))
        at_step(t, CELLS_MORE, 2, lambda n: two_tiles(1, n))
        at_step(t, REDUCE, 8, reduce_start)
        at_step(t, ROWS, 1, row_far)
        at_step(t, ROWS + 1, 1, row_east)
        at_step(t, ROWS + 2, 1, row_west)
        at_step(t, ROWS + 3, 1, row_own)
        at_step(t, ROWS + 6, 1, row_update)
        return 0

    lax.fori_loop(0, REDUCE_HOME + 8, step, 0)
    sums_copy(1).wait()
    for j in (0, 1, 2, 4, 5, 6, 7):
        home_copy(j).wait_recv()
    for lane in range(0, D, 128):
        at = slice(lane, lane + 128)
        grad = col_grad[:, at]
        for j in (0, 1, 2, 4, 5, 6, 7):
            grad = grad + recv_z[j, :, at].astype(F32)
        sums = col_sums[:, at] + grad * grad
        made[2 * QUARTER : 2 * QUARTER + PIECE, at] = (
            col_local[:, at] - learn_rate * grad * lax.rsqrt(sums)
        )
        made[2 * QUARTER + PIECE :, at] = sums
    result_copy(1).start()

    for j in range(1, NZ):
        z_copy(j).wait_send()

    def drain(j, _):
        for up in (True, False):
            y_copy(j, up).wait_send()
            y_forward(j, up).wait_send()
            half_copy(j, up).wait_send()
            full_copy(j, up).wait_send()
        mate_copy(j).wait_send()
        mate_send(j).wait_send()

        @pl.when(j != 3)
        def _():
            home_copy(j).wait_send()

        return 0

    lax.fori_loop(0, NZ, drain, 0)
    for j in range(6):
        x_copy(j).wait_send()
    for up in (True, False):
        xhalf(up).wait_send()
        xfull(up).wait_send()
    for i in range(2):
        result_copy(i).wait()


def split_kernel(result, row_new, row_accum_new, col_new, col_accum_new, held, sem):
    reads, writes = [], []
    first = 0
    for i, out in enumerate((row_new, row_accum_new, col_new, col_accum_new)):
        at = pl.ds(first, out.shape[0])
        reads.append(pltpu.make_async_copy(result.at[at], held.at[at], sem.at[i]))
        writes.append(pltpu.make_async_copy(held.at[at], out, sem.at[4 + i]))
        first += out.shape[0]
    for read in reads:
        read.start()
    for read, write in zip(reads, writes):
        read.wait()
        write.start()
    for write in writes:
        write.wait()


def body(
    row_embed,
    row_accum,
    col_embed,
    col_accum,
    col_freq,
    row_freq,
    block_cols,
    counts,
    excluded,
    log_total,
):
    vmem = pl.BlockSpec(memory_space=pltpu.VMEM)
    smem = pl.BlockSpec(memory_space=pltpu.SMEM)
    hbm = pl.BlockSpec(memory_space=pl.ANY)
    row_shape = jax.ShapeDtypeStruct((QUARTER, D), F32)
    col_shape = jax.ShapeDtypeStruct((PIECE, D), F32)
    result = pl.pallas_call(
        step_kernel,
        out_shape=jax.ShapeDtypeStruct((2 * QUARTER + 2 * PIECE, D), F32),
        in_specs=[smem, smem, vmem, vmem, vmem, vmem, vmem, hbm, hbm, hbm],
        out_specs=hbm,
        scratch_shapes=[
            pltpu.VMEM((2 * QUARTER + 2 * PIECE, D), F32),
            pltpu.VMEM((QUARTER, D), F32),
            pltpu.VMEM((PIECE, D), F32),
            pltpu.VMEM((QUARTER, D), F32),
            pltpu.VMEM((PIECE, D), F32),
            pltpu.VMEM((QUARTER, 128), F32),
            pltpu.VMEM((NZ, NY, NK, PIECE, D), BF16),
            pltpu.VMEM((2, 2, 2, QUARTER, D), BF16),
            pltpu.VMEM((BLOCK, D), BF16),
            pltpu.VMEM((2, 2, BLOCK, HALF), jnp.int32),
            pltpu.VMEM((2, 2, BLOCK, HALF), F32),
            pltpu.VMEM((2, 2, BLOCK, HALF), F32),
            pltpu.VMEM((2, 2, BLOCK, HALF), BF16),
            pltpu.VMEM((BLOCK, 128), F32),
            pltpu.VMEM((NZ, NY, NK, PIECE, D), F32),
            pltpu.VMEM((NZ, NY, PIECE, D), F32),
            pltpu.VMEM((2, NZ, PIECE // 2, D), BF16),
            pltpu.VMEM((2, NZ, PIECE // 2, D), BF16),
            pltpu.VMEM((2, NZ, PIECE, D), BF16),
            pltpu.VMEM((2, NZ, PIECE, D), BF16),
            pltpu.VMEM((NZ, PIECE, D), BF16),
            pltpu.VMEM((NZ, PIECE, D), BF16),
            pltpu.VMEM((2, 128, D), BF16),
            pltpu.VMEM((2, 128, D), BF16),
            pltpu.VMEM((2, QUARTER, D), BF16),
            pltpu.VMEM((2, QUARTER, D), BF16),
            pltpu.SemaphoreType.DMA((12,)),
            pltpu.SemaphoreType.DMA((6, NZ)),
            pltpu.SemaphoreType.DMA((6, NZ)),
            pltpu.SemaphoreType.DMA((6, NZ)),
            pltpu.SemaphoreType.DMA((6, NZ)),
            pltpu.SemaphoreType.DMA((10,)),
            pltpu.SemaphoreType.DMA((10,)),
        ],
        compiler_params=pltpu.CompilerParams(
            collective_id=0, has_side_effects=True, vmem_limit_bytes=58 << 20
        ),
        cost_estimate=pl.CostEstimate(
            flops=8 << 30, bytes_accessed=12 << 20, transcendentals=8 << 20
        ),
        name="swivel_step",
    )(
        block_cols.reshape(2),
        log_total.reshape(1),
        row_embed,
        col_embed[0],
        row_freq.reshape(1, BLOCK),
        col_freq,
        excluded.reshape(1, EXCLUDED),
        row_accum,
        col_accum[0],
        counts[0, 0],
    )
    row_new, row_accum_new, col_new, col_accum_new = pl.pallas_call(
        split_kernel,
        out_shape=(row_shape, row_shape, col_shape, col_shape),
        in_specs=[hbm],
        out_specs=(hbm, hbm, hbm, hbm),
        scratch_shapes=[
            pltpu.VMEM((2 * QUARTER + 2 * PIECE, D), F32),
            pltpu.SemaphoreType.DMA((8,)),
        ],
        name="split_result",
    )(result)
    return (row_new, row_accum_new, col_new[None], col_accum_new[None])


def solution(mesh):
    in_specs = (
        P(("row", "col"), None),
        P(("row", "col"), None),
        P("col", "row", None),
        P("col", "row", None),
        P("col", None),
        P("row"),
        P("row", "col", None),
        P("row", "col", None, None, None),
        P(),
        P(),
    )
    out_specs = (
        P(("row", "col"), None),
        P(("row", "col"), None),
        P("col", "row", None),
        P("col", "row", None),
    )
    return jax.shard_map(body, mesh=mesh, in_specs=in_specs, out_specs=out_specs, check_vma=False)
```

```python
import jax
import jax.numpy as jnp
from jax import lax
from jax.experimental import pallas as pl
from jax.experimental.pallas import tpu as pltpu
from jax.sharding import PartitionSpec as P

MESH = pl.DeviceIdType.MESH
NX, NY, NZ, NK = 4, 4, 8, 2
BLOCK = 1024
HALF = 512
EXCLUDED = 512
PIECE = 64
QUARTER = 256
D = 512
F32 = jnp.float32
BF16 = jnp.bfloat16

learn_rate = 0.2
decay_rate = 0.5

GATHER_ORDER = (1, 7, 3, 5, 0, 2, 6, 4)
REDUCE_ORDER = (3, 5, 1, 7, 4, 2, 6, 0)
OWN_IN = GATHER_ORDER.index(0)
OWN_OUT = REDUCE_ORDER.index(0)
FIRST = GATHER_ORDER[1] % 2
OTHERS = tuple(j for j in range(NZ) if j != OWN_OUT)

GATHER_MORE = 1
GATHER_NEAR = 2
GATHER_FAR = 4
CELLS = 8
REDUCE = 10
CELLS_MORE = REDUCE + 2
REDUCE_FAR = REDUCE + 2
REDUCE_NEAR = REDUCE + 4
REDUCE_HOME = REDUCE + 6
ROWS = REDUCE + 5


def pick(index, values):
    result = jnp.int32(values[-1])
    for place in range(len(values) - 1):
        result = jnp.where(index == place, jnp.int32(values[place]), result)
    return result


def step_kernel(
    chosen, total, row_in, col_in, row_freq_in, col_freq_in, excluded_in, row_accum, col_accum, counts,
    result,
    row_local, col_local, row_freq, col_freq, excluded,
    made, own_grad, col_grad, row_sums, col_sums, decay,
    cols, mine, rows, cnt, wgt, base, cells, row_logs,
    part, pair_in, send_half, recv_half, send_full, recv_full, send_z, recv_z,
    xsend_half, xrecv_half, xsend_full, xrecv_full,
    cnt_sem, ag_s, ag_r, rs_s, rs_r, x_s, x_r,
):
    r = lax.axis_index("row")
    x = lax.axis_index("col")
    k = lax.rem(r, NK)
    y = lax.rem(r // NK, NY)
    z = r // (NK * NY)
    yp, ym, y2 = lax.rem(y + 1, NY), lax.rem(y + 3, NY), lax.rem(y + 2, NY)
    xp, xm, x2 = lax.rem(x + 1, NX), lax.rem(x + 3, NX), lax.rem(x + 2, NX)
    other = 1 - k

    def dev(dx, dy, dz, dk):
        return ((dz * NY + dy) * NK + dk, dx)

    right, left = dev(x, yp, z, k), dev(x, ym, z, k)
    east, west = dev(xp, y, z, k), dev(xm, y, z, k)
    mate = dev(x, y, z, other)

    def remote(src, dst, s, q, target):
        return pltpu.make_async_remote_copy(
            src_ref=src, dst_ref=dst, send_sem=s, recv_sem=q, device_id=target, device_id_type=MESH
        )

    def count_copy(c):
        h, s, b = c // 4, (c // 2) % 2, c % 2
        lane = pl.multiple_of(lax.rem(z + h + FIRST, 2) * HALF, HALF)
        return pltpu.make_async_copy(
            counts.at[s, pl.ds(b * HALF, HALF), pl.ds(lane, HALF)],
            cnt.at[s, h, pl.ds(b * HALF, HALF)],
            cnt_sem.at[c],
        )

    def sums_copy(i):
        return pltpu.make_async_copy(
            (row_accum, col_accum)[i], (row_sums, col_sums)[i], cnt_sem.at[8 + i]
        )

    barrier = pltpu.get_barrier_semaphore()
    for target in (right, left, east, west, mate):
        pl.semaphore_signal(barrier, inc=1, device_id=target, device_id_type=MESH)
    for dz in range(1, NZ):
        pl.semaphore_signal(
            barrier, inc=1, device_id=dev(x, y, lax.rem(z + dz, NZ), k), device_id_type=MESH
        )
    sources = (col_in, row_in, row_freq_in, col_freq_in, excluded_in)
    targets = (col_local, row_local, row_freq, col_freq, excluded)
    for i in range(5):
        pltpu.make_async_copy(sources[i], targets[i], cnt_sem.at[12 + i]).start()

    for c in range(8):
        count_copy(c).start()
    for i in range(2):
        sums_copy(i).start()

    def ready(i):
        pltpu.make_async_copy(sources[i], targets[i], cnt_sem.at[12 + i]).wait()

    ready(0)
    cols[z, y, k] = col_local[...].astype(BF16)
    my_rows = pl.multiple_of(x * QUARTER, QUARTER)
    ready(1)
    rows[pl.ds(my_rows, QUARTER)] = row_local[...].astype(BF16)
    pl.semaphore_wait(barrier, 5 + NZ - 1)

    def z_copy(i):
        zt = lax.rem(z + pick(i, GATHER_ORDER), NZ)
        return remote(cols.at[z, y, k], cols.at[z, y, k], ag_s.at[0, i], ag_r.at[0, z], dev(x, y, zt, k))

    def z_arrival(zs):
        return remote(cols.at[zs, y, k], cols.at[zs, y, k], ag_s.at[0, 0], ag_r.at[0, zs], mate)

    def y_copy(zs, up):
        kind, target = (1, right) if up else (2, left)
        return remote(cols.at[zs, y, k], cols.at[zs, y, k], ag_s.at[kind, zs], ag_r.at[kind, zs], target)

    def y_arrival(zs, up):
        kind, src = (1, ym) if up else (2, yp)
        return remote(cols.at[zs, src, k], cols.at[zs, src, k], ag_s.at[kind, zs], ag_r.at[kind, zs], mate)

    def y_forward(zs, up):
        kind, src, start, target = (3, ym, 0, right) if up else (4, yp, PIECE // 2, left)
        ref = cols.at[zs, src, k, pl.ds(start, PIECE // 2)]
        return remote(ref, ref, ag_s.at[kind, zs], ag_r.at[kind, zs], target)

    def y_far(zs, up):
        kind, start = (3, 0) if up else (4, PIECE // 2)
        ref = cols.at[zs, y2, k, pl.ds(start, PIECE // 2)]
        return remote(ref, ref, ag_s.at[kind, zs], ag_r.at[kind, zs], mate)

    def mate_copy(zs):
        return remote(cols.at[zs, :, k], cols.at[zs, :, k], ag_s.at[5, zs], ag_r.at[5, zs], mate)

    def mate_arrival(zs):
        return remote(cols.at[zs, :, other], cols.at[zs, :, other], ag_s.at[5, zs], ag_r.at[5, zs], mate)

    def quarter(q, start, size):
        return rows.at[pl.ds(pl.multiple_of(q * QUARTER + start, 128), size)]

    def x_copy(i):
        n = 128
        q, start, target = ((x, 0, east), (x, n, west), (x, n, east), (x, 0, west), (xm, 0, east), (xp, n, west))[i]
        return remote(quarter(q, start, n), quarter(q, start, n), x_s.at[i], x_r.at[i], target)

    def x_arrival(i):
        n = 128
        q, start = ((xm, 0), (xp, n), (xm, n), (xp, 0), (x2, 0), (x2, n))[i]
        return remote(quarter(q, start, n), quarter(q, start, n), x_s.at[i], x_r.at[i], mate)

    y_copy(z, True).start()
    y_copy(z, False).start()
    for i in range(4):
        if i != OWN_IN:
            z_copy(i).start()
    for i in range(4):
        x_copy(i).start()

    for i in range(2, 5):
        ready(i)
    logs = jnp.log(row_freq[...].astype(F32)) - total[0]
    row_logs[...] = jnp.broadcast_to(logs, (128, BLOCK)).T

    ids = r * BLOCK + my_rows + lax.broadcasted_iota(jnp.int32, (QUARTER, EXCLUDED), 0)
    listed = jnp.max(jnp.where(ids == excluded[...], 1.0, 0.0), axis=1, keepdims=True)
    root = jnp.sqrt(row_freq[:, pl.ds(my_rows, QUARTER)].astype(F32))
    coef = jnp.broadcast_to(decay_rate * root / (root + 30.0), (128, QUARTER)).T
    decay[...] = jnp.where(listed > 0.0, 0.0, coef)

    def of_block(block, options):
        result = options[3]
        for b in range(3):
            result = lax.select(block == b, options[b], result)
        return result

    def prepare(c):
        h, s = c // 4, lax.rem(c // 2, 2)
        first = lax.rem(c, 2) * HALF
        ref = cnt.at[s, h, pl.ds(first, HALF)]
        pltpu.make_async_copy(ref, ref, cnt_sem.at[c]).wait()
        parity = lax.rem(z + h + FIRST, 2)
        freq = of_block(
            chosen[s],
            [col_freq[:, pl.ds(pl.multiple_of(b * BLOCK + parity * HALF, HALF), HALF)] for b in range(4)],
        )
        col_logs = jnp.log(freq.astype(F32))

        def tile(n, _):
            at = pl.ds(pl.multiple_of(first + n * PIECE, PIECE), PIECE)
            rl = row_logs[at]
            for lane in range(0, HALF, 128):
                count = cnt[s, h, at, lane : lane + 128]
                full = count > 0
                value = jnp.maximum(count, 1).astype(F32)
                root = value * lax.rsqrt(value)
                base[s, h, at, lane : lane + 128] = (rl + col_logs[:, lane : lane + 128]) - jnp.log(value)
                wgt[s, h, at, lane : lane + 128] = jnp.where(
                    full, (0.1 / BLOCK) + (0.25 / BLOCK) * root, 0.0
                )
            return 0

        lax.fori_loop(0, HALF // PIECE, tile, 0)

    def cell_tile(h, n):
        s, q = n // 2, lax.rem(n, 2)
        parity = lax.rem(z + h + FIRST, 2)
        col_tile = of_block(
            chosen[s], [cols[2 * b + parity, pl.ds(2 * q, 2)].reshape(QUARTER, D) for b in range(4)]
        )
        mine[s, h, q] = col_tile
        lane = pl.multiple_of(q * QUARTER, QUARTER)
        for m in range(4):
            at = pl.ds(m * QUARTER, QUARTER)
            predicted = lax.dot_general(
                rows[at], col_tile, (((1,), (1,)), ((), ())), preferred_element_type=F32
            )
            shifted = predicted + base[s, h, at, pl.ds(lane, QUARTER)]
            w = wgt[s, h, at, pl.ds(lane, QUARTER)]
            hinge = 1.0 / (BLOCK + BLOCK * jnp.exp(-shifted))
            cells[s, h, at, pl.ds(lane, QUARTER)] = jnp.where(w > 0.0, w * shifted, hinge).astype(BF16)

    def mate_send(i):
        return remote(part.at[i, :, other], pair_in.at[i], rs_s.at[0, i], rs_r.at[0, i], mate)

    def mate_recv(i):
        return remote(pair_in.at[i], pair_in.at[i], rs_s.at[0, i], rs_r.at[0, i], mate)

    def half_copy(i, up):
        n, target = (0, right) if up else (1, left)
        return remote(send_half.at[n, i], recv_half.at[n, i], rs_s.at[1 + n, i], rs_r.at[1 + n, i], target)

    def full_copy(i, up):
        n, target = (0, right) if up else (1, left)
        return remote(send_full.at[n, i], recv_full.at[n, i], rs_s.at[3 + n, i], rs_r.at[3 + n, i], target)

    def home_copy(i):
        zt = lax.rem(z + pick(i, REDUCE_ORDER), NZ)
        return remote(send_z.at[i], recv_z.at[i], rs_s.at[5, i], rs_r.at[5, i], dev(x, y, zt, k))

    def chip_sum(i, dest):
        return part[i, dest, k] + pair_in[i, dest]

    def col_part(i):
        shift = pick(i, REDUCE_ORDER)
        zt = lax.rem(z + shift, NZ)
        h = lax.rem(shift + FIRST, 2)
        b = zt // 2
        for q in range(2):
            lanes = slice(q * QUARTER, (q + 1) * QUARTER)
            cell = lax.select(chosen[1] == b, cells[1, h, :, lanes], jnp.zeros((BLOCK, QUARTER), BF16))
            found = lax.dot_general(
                lax.select(chosen[0] == b, cells[0, h, :, lanes], cell),
                rows[...],
                (((0,), (0,)), ((), ())),
                preferred_element_type=F32,
            )
            part[i, 2 * q : 2 * q + 2] = found.reshape(2, NK, PIECE, D)

    def row_part(q):
        at = pl.ds(pl.multiple_of(q * QUARTER, QUARTER), QUARTER)
        result = jnp.zeros((QUARTER, D), F32)
        for s in range(2):
            for h in range(2):
                result = result + jnp.dot(
                    cells[s, h, at], mine[s, h].reshape(HALF, D), preferred_element_type=F32
                )
        return result

    def xhalf(up):
        n, target = (0, east) if up else (1, west)
        return remote(xsend_half.at[n], xrecv_half.at[n], x_s.at[6 + n], x_r.at[6 + n], target)

    def xfull(up):
        n, target = (0, east) if up else (1, west)
        return remote(xsend_full.at[n], xrecv_full.at[n], x_s.at[8 + n], x_r.at[8 + n], target)

    lower = PIECE // 2

    def at_step(t, first, count, work):
        @pl.when((t >= first) & (t < first + count))
        def _():
            work(t - first)

    def gather_z(i):
        zs = lax.rem(z + pick(i, GATHER_ORDER), NZ)

        @pl.when(i != OWN_IN)
        def _():
            z_arrival(zs).wait_recv()
            y_copy(zs, True).start()
            y_copy(zs, False).start()

    def gather_more(i):
        @pl.when(4 + i != OWN_IN)
        def _():
            z_copy(4 + i).start()

    def gather_near(i):
        zs = lax.rem(z + pick(i, GATHER_ORDER), NZ)
        y_arrival(zs, True).wait_recv()
        y_forward(zs, True).start()
        y_arrival(zs, False).wait_recv()
        y_forward(zs, False).start()

    def gather_far(i):
        zs = lax.rem(z + pick(i, GATHER_ORDER), NZ)
        y_far(zs, True).wait_recv()
        y_far(zs, False).wait_recv()
        mate_copy(zs).start()

    def gather_rows(_):
        for j in range(2):
            x_arrival(j).wait_recv()
            x_copy(4 + j).start()

    def half_ready(h):
        for j in range(4):
            mate_arrival(lax.rem(z + GATHER_ORDER[4 * h + j], NZ)).wait_recv()

    def rows_ready(_):
        for j in range(2, 6):
            x_arrival(j).wait_recv()

    def prepare_two(i):
        prepare(2 * i)
        prepare(2 * i + 1)

    def two_tiles(h, n):
        cell_tile(h, 2 * n)
        cell_tile(h, 2 * n + 1)

    def reduce_start(i):
        col_part(i)
        mate_send(i).start()

    def reduce_far(j):
        mate_recv(j).wait_recv()
        value = chip_sum(j, y2).astype(BF16)
        send_half[0, j] = value[:lower]
        half_copy(j, True).start()
        send_half[1, j] = value[lower:]
        half_copy(j, False).start()

    def reduce_near(j):
        half_copy(j, True).wait_recv()
        value = chip_sum(j, yp)
        send_full[0, j, :lower] = (value[:lower] + recv_half[0, j].astype(F32)).astype(BF16)
        send_full[0, j, lower:] = value[lower:].astype(BF16)
        full_copy(j, True).start()
        half_copy(j, False).wait_recv()
        value = chip_sum(j, ym)
        send_full[1, j, :lower] = value[:lower].astype(BF16)
        send_full[1, j, lower:] = (value[lower:] + recv_half[1, j].astype(F32)).astype(BF16)
        full_copy(j, False).start()

    def reduce_home(j):
        full_copy(j, True).wait_recv()
        full_copy(j, False).wait_recv()
        value = chip_sum(j, y) + recv_full[0, j].astype(F32) + recv_full[1, j].astype(F32)

        @pl.when(j == OWN_OUT)
        def _():
            col_grad[...] = value

        @pl.when(j != OWN_OUT)
        def _():
            send_z[j] = value.astype(BF16)
            home_copy(j).start()

    def row_far(_):
        value = row_part(x2).astype(BF16)
        xsend_half[0] = value[:128]
        xsend_half[1] = value[128:]
        xhalf(True).start()
        xhalf(False).start()

    def row_east(_):
        value = row_part(xp)
        xhalf(True).wait_recv()
        xsend_full[0, :128] = (value[:128] + xrecv_half[0].astype(F32)).astype(BF16)
        xsend_full[0, 128:] = value[128:].astype(BF16)
        xfull(True).start()

    def row_west(_):
        value = row_part(xm)
        xhalf(False).wait_recv()
        xsend_full[1, :128] = value[:128].astype(BF16)
        xsend_full[1, 128:] = (value[128:] + xrecv_half[1].astype(F32)).astype(BF16)
        xfull(False).start()

    def row_own(_):
        own_grad[...] = row_part(x)

    def result_copy(i):
        at = pl.ds((0, 2 * QUARTER)[i], (2 * QUARTER, 2 * PIECE)[i])
        return pltpu.make_async_copy(made.at[at], result.at[at], cnt_sem.at[10 + i])

    def row_update(_):
        sums_copy(0).wait()
        xfull(True).wait_recv()
        xfull(False).wait_recv()
        for lane in range(0, D, 128):
            at = slice(lane, lane + 128)
            value = row_local[:, at]
            grad = own_grad[:, at] + xrecv_full[0, :, at].astype(F32) + xrecv_full[1, :, at].astype(F32)
            grad = grad + decay[...] * value
            sums = row_sums[:, at] + grad * grad
            made[:QUARTER, at] = value - learn_rate * grad * lax.rsqrt(sums)
            made[QUARTER : 2 * QUARTER, at] = sums
        result_copy(0).start()

    def step(t, _):
        at_step(t, 0, 8, gather_z)
        at_step(t, GATHER_MORE, 4, gather_more)
        at_step(t, GATHER_NEAR, 8, gather_near)
        at_step(t, GATHER_FAR, 8, gather_far)
        at_step(t, 2, 1, gather_rows)
        at_step(t, REDUCE_HOME, 8, reduce_home)
        at_step(t, REDUCE_NEAR, 8, reduce_near)
        at_step(t, REDUCE_FAR, 8, reduce_far)
        at_step(t, 0, 4, prepare_two)
        at_step(t, CELLS, 1, rows_ready)
        at_step(t, CELLS, 1, lambda _: half_ready(0))
        at_step(t, CELLS, 2, lambda n: two_tiles(0, n))
        at_step(t, CELLS_MORE, 1, lambda _: half_ready(1))
        at_step(t, CELLS_MORE, 2, lambda n: two_tiles(1, n))
        at_step(t, REDUCE, 8, reduce_start)
        at_step(t, ROWS, 1, row_far)
        at_step(t, ROWS + 1, 1, row_east)
        at_step(t, ROWS + 2, 1, row_west)
        at_step(t, ROWS + 3, 1, row_own)
        at_step(t, ROWS + 6, 1, row_update)
        return 0

    lax.fori_loop(0, REDUCE_HOME + 8, step, 0)
    sums_copy(1).wait()
    for j in OTHERS:
        home_copy(j).wait_recv()
    for lane in range(0, D, 128):
        at = slice(lane, lane + 128)
        grad = col_grad[:, at]
        for j in OTHERS:
            grad = grad + recv_z[j, :, at].astype(F32)
        sums = col_sums[:, at] + grad * grad
        made[2 * QUARTER : 2 * QUARTER + PIECE, at] = (
            col_local[:, at] - learn_rate * grad * lax.rsqrt(sums)
        )
        made[2 * QUARTER + PIECE :, at] = sums
    result_copy(1).start()

    for j in range(NZ):
        if j != OWN_IN:
            z_copy(j).wait_send()

    def drain(j, _):
        for up in (True, False):
            y_copy(j, up).wait_send()
            y_forward(j, up).wait_send()
            half_copy(j, up).wait_send()
            full_copy(j, up).wait_send()
        mate_copy(j).wait_send()
        mate_send(j).wait_send()

        @pl.when(j != OWN_OUT)
        def _():
            home_copy(j).wait_send()

        return 0

    lax.fori_loop(0, NZ, drain, 0)
    for j in range(6):
        x_copy(j).wait_send()
    for up in (True, False):
        xhalf(up).wait_send()
        xfull(up).wait_send()
    for i in range(2):
        result_copy(i).wait()


def split_kernel(result, row_new, row_accum_new, col_new, col_accum_new, held, sem):
    reads, writes = [], []
    first = 0
    for i, out in enumerate((row_new, row_accum_new, col_new, col_accum_new)):
        at = pl.ds(first, out.shape[0])
        reads.append(pltpu.make_async_copy(result.at[at], held.at[at], sem.at[i]))
        writes.append(pltpu.make_async_copy(held.at[at], out, sem.at[4 + i]))
        first += out.shape[0]
    for read in reads:
        read.start()
    for read, write in zip(reads, writes):
        read.wait()
        write.start()
    for write in writes:
        write.wait()


def body(
    row_embed,
    row_accum,
    col_embed,
    col_accum,
    col_freq,
    row_freq,
    block_cols,
    counts,
    excluded,
    log_total,
):
    smem = pl.BlockSpec(memory_space=pltpu.SMEM)
    hbm = pl.BlockSpec(memory_space=pl.ANY)
    row_shape = jax.ShapeDtypeStruct((QUARTER, D), F32)
    col_shape = jax.ShapeDtypeStruct((PIECE, D), F32)
    result = pl.pallas_call(
        step_kernel,
        out_shape=jax.ShapeDtypeStruct((2 * QUARTER + 2 * PIECE, D), F32),
        in_specs=[smem, smem] + [hbm] * 8,
        out_specs=hbm,
        scratch_shapes=[
            pltpu.VMEM((QUARTER, D), F32),
            pltpu.VMEM((PIECE, D), F32),
            pltpu.VMEM((1, BLOCK), jnp.int32),
            pltpu.VMEM((1, NY * BLOCK), jnp.int32),
            pltpu.VMEM((1, EXCLUDED), jnp.int32),
            pltpu.VMEM((2 * QUARTER + 2 * PIECE, D), F32),
            pltpu.VMEM((QUARTER, D), F32),
            pltpu.VMEM((PIECE, D), F32),
            pltpu.VMEM((QUARTER, D), F32),
            pltpu.VMEM((PIECE, D), F32),
            pltpu.VMEM((QUARTER, 128), F32),
            pltpu.VMEM((NZ, NY, NK, PIECE, D), BF16),
            pltpu.VMEM((2, 2, 2, QUARTER, D), BF16),
            pltpu.VMEM((BLOCK, D), BF16),
            pltpu.VMEM((2, 2, BLOCK, HALF), jnp.int32),
            pltpu.VMEM((2, 2, BLOCK, HALF), F32),
            pltpu.VMEM((2, 2, BLOCK, HALF), F32),
            pltpu.VMEM((2, 2, BLOCK, HALF), BF16),
            pltpu.VMEM((BLOCK, 128), F32),
            pltpu.VMEM((NZ, NY, NK, PIECE, D), F32),
            pltpu.VMEM((NZ, NY, PIECE, D), F32),
            pltpu.VMEM((2, NZ, PIECE // 2, D), BF16),
            pltpu.VMEM((2, NZ, PIECE // 2, D), BF16),
            pltpu.VMEM((2, NZ, PIECE, D), BF16),
            pltpu.VMEM((2, NZ, PIECE, D), BF16),
            pltpu.VMEM((NZ, PIECE, D), BF16),
            pltpu.VMEM((NZ, PIECE, D), BF16),
            pltpu.VMEM((2, 128, D), BF16),
            pltpu.VMEM((2, 128, D), BF16),
            pltpu.VMEM((2, QUARTER, D), BF16),
            pltpu.VMEM((2, QUARTER, D), BF16),
            pltpu.SemaphoreType.DMA((17,)),
            pltpu.SemaphoreType.DMA((6, NZ)),
            pltpu.SemaphoreType.DMA((6, NZ)),
            pltpu.SemaphoreType.DMA((6, NZ)),
            pltpu.SemaphoreType.DMA((6, NZ)),
            pltpu.SemaphoreType.DMA((10,)),
            pltpu.SemaphoreType.DMA((10,)),
        ],
        compiler_params=pltpu.CompilerParams(
            collective_id=0, has_side_effects=True, vmem_limit_bytes=58 << 20
        ),
        cost_estimate=pl.CostEstimate(
            flops=8 << 30, bytes_accessed=12 << 20, transcendentals=8 << 20
        ),
        name="swivel_step",
    )(
        block_cols.reshape(2),
        log_total.reshape(1),
        row_embed,
        col_embed[0],
        row_freq.reshape(1, BLOCK),
        col_freq,
        excluded.reshape(1, EXCLUDED),
        row_accum,
        col_accum[0],
        counts[0, 0],
    )
    row_new, row_accum_new, col_new, col_accum_new = pl.pallas_call(
        split_kernel,
        out_shape=(row_shape, row_shape, col_shape, col_shape),
        in_specs=[hbm],
        out_specs=(hbm, hbm, hbm, hbm),
        scratch_shapes=[
            pltpu.VMEM((2 * QUARTER + 2 * PIECE, D), F32),
            pltpu.SemaphoreType.DMA((8,)),
        ],
        name="split_result",
    )(result)
    return (row_new, row_accum_new, col_new[None], col_accum_new[None])


def solution(mesh):
    in_specs = (
        P(("row", "col"), None),
        P(("row", "col"), None),
        P("col", "row", None),
        P("col", "row", None),
        P("col", None),
        P("row"),
        P("row", "col", None),
        P("row", "col", None, None, None),
        P(),
        P(),
    )
    out_specs = (
        P(("row", "col"), None),
        P(("row", "col"), None),
        P("col", "row", None),
        P("col", "row", None),
    )
    return jax.shard_map(body, mesh=mesh, in_specs=in_specs, out_specs=out_specs, check_vma=False)
```

```python
import jax
import jax.numpy as jnp
from jax import lax
from jax.experimental import pallas as pl
from jax.experimental.pallas import tpu as pltpu
from jax.sharding import PartitionSpec as P

MESH = pl.DeviceIdType.MESH
NX, NY, NZ, NK = 4, 4, 8, 2
BLOCK = 1024
HALF = 512
EXCLUDED = 512
PIECE = 64
QUARTER = 256
D = 512
F32 = jnp.float32
BF16 = jnp.bfloat16

learn_rate = 0.2
decay_rate = 0.5

GATHER_ORDER = (1, 7, 3, 5, 0, 2, 6, 4)
REDUCE_ORDER = (3, 5, 1, 7, 4, 2, 6, 0)
OWN_IN = GATHER_ORDER.index(0)
OWN_OUT = REDUCE_ORDER.index(0)
FIRST = GATHER_ORDER[1] % 2
OTHERS = tuple(j for j in range(NZ) if j != OWN_OUT)

GATHER_MORE = 1
GATHER_NEAR = 2
GATHER_FAR = 4
CELLS = 8
REDUCE = 10
CELLS_MORE = REDUCE + 2
REDUCE_FAR = REDUCE + 2
REDUCE_NEAR = REDUCE + 4
REDUCE_HOME = REDUCE + 6
ROWS = REDUCE + 5


def pick(index, values):
    result = jnp.int32(values[-1])
    for place in range(len(values) - 1):
        result = jnp.where(index == place, jnp.int32(values[place]), result)
    return result


def step_kernel(
    chosen, total, row_in, col_in, row_freq_in, col_freq_in, excluded_in, row_accum, col_accum, counts,
    result,
    row_local, col_local, row_freq, col_freq, excluded,
    made, own_grad, col_grad, row_sums, col_sums, decay,
    cols, mine, rows, cnt, wgt, base, cells, row_logs,
    part, pair_in, send_half, recv_half, send_full, recv_full, send_z, recv_z,
    xsend_half, xrecv_half, xsend_full, xrecv_full,
    cnt_sem, ag_s, ag_r, rs_s, rs_r, x_s, x_r,
):
    r = lax.axis_index("row")
    x = lax.axis_index("col")
    k = lax.rem(r, NK)
    y = lax.rem(r // NK, NY)
    z = r // (NK * NY)
    yp, ym, y2 = lax.rem(y + 1, NY), lax.rem(y + 3, NY), lax.rem(y + 2, NY)
    xp, xm, x2 = lax.rem(x + 1, NX), lax.rem(x + 3, NX), lax.rem(x + 2, NX)
    other = 1 - k

    def dev(dx, dy, dz, dk):
        return ((dz * NY + dy) * NK + dk, dx)

    right, left = dev(x, yp, z, k), dev(x, ym, z, k)
    east, west = dev(xp, y, z, k), dev(xm, y, z, k)
    mate = dev(x, y, z, other)

    def remote(src, dst, s, q, target):
        return pltpu.make_async_remote_copy(
            src_ref=src, dst_ref=dst, send_sem=s, recv_sem=q, device_id=target, device_id_type=MESH
        )

    def count_copy(c):
        h, s, b = c // 4, (c // 2) % 2, c % 2
        lane = pl.multiple_of(lax.rem(z + h + FIRST, 2) * HALF, HALF)
        return pltpu.make_async_copy(
            counts.at[s, pl.ds(b * HALF, HALF), pl.ds(lane, HALF)],
            cnt.at[s, h, pl.ds(b * HALF, HALF)],
            cnt_sem.at[c],
        )

    def sums_copy(i):
        return pltpu.make_async_copy(
            (row_accum, col_accum)[i], (row_sums, col_sums)[i], cnt_sem.at[8 + i]
        )

    barrier = pltpu.get_barrier_semaphore()
    for target in (right, left, east, west, mate):
        pl.semaphore_signal(barrier, inc=1, device_id=target, device_id_type=MESH)
    for dz in range(1, NZ):
        pl.semaphore_signal(
            barrier, inc=1, device_id=dev(x, y, lax.rem(z + dz, NZ), k), device_id_type=MESH
        )
    sources = (col_in, row_in, row_freq_in, col_freq_in, excluded_in)
    targets = (col_local, row_local, row_freq, col_freq, excluded)
    for i in range(5):
        pltpu.make_async_copy(sources[i], targets[i], cnt_sem.at[12 + i]).start()

    for c in range(8):
        count_copy(c).start()
    for i in range(2):
        sums_copy(i).start()

    def ready(i):
        pltpu.make_async_copy(sources[i], targets[i], cnt_sem.at[12 + i]).wait()

    ready(0)
    cols[z, y, k] = col_local[...].astype(BF16)
    my_rows = pl.multiple_of(x * QUARTER, QUARTER)
    ready(1)
    rows[pl.ds(my_rows, QUARTER)] = row_local[...].astype(BF16)
    pl.semaphore_wait(barrier, 5 + NZ - 1)

    def z_copy(i):
        zt = lax.rem(z + pick(i, GATHER_ORDER), NZ)
        return remote(cols.at[z, y, k], cols.at[z, y, k], ag_s.at[0, i], ag_r.at[0, z], dev(x, y, zt, k))

    def z_arrival(zs):
        return remote(cols.at[zs, y, k], cols.at[zs, y, k], ag_s.at[0, 0], ag_r.at[0, zs], mate)

    def y_copy(zs, up):
        kind, target = (1, right) if up else (2, left)
        return remote(cols.at[zs, y, k], cols.at[zs, y, k], ag_s.at[kind, zs], ag_r.at[kind, zs], target)

    def y_arrival(zs, up):
        kind, src = (1, ym) if up else (2, yp)
        return remote(cols.at[zs, src, k], cols.at[zs, src, k], ag_s.at[kind, zs], ag_r.at[kind, zs], mate)

    def y_forward(zs, up):
        kind, src, start, target = (3, ym, 0, right) if up else (4, yp, PIECE // 2, left)
        ref = cols.at[zs, src, k, pl.ds(start, PIECE // 2)]
        return remote(ref, ref, ag_s.at[kind, zs], ag_r.at[kind, zs], target)

    def y_far(zs, up):
        kind, start = (3, 0) if up else (4, PIECE // 2)
        ref = cols.at[zs, y2, k, pl.ds(start, PIECE // 2)]
        return remote(ref, ref, ag_s.at[kind, zs], ag_r.at[kind, zs], mate)

    def mate_copy(zs):
        return remote(cols.at[zs, :, k], cols.at[zs, :, k], ag_s.at[5, zs], ag_r.at[5, zs], mate)

    def mate_arrival(zs):
        return remote(cols.at[zs, :, other], cols.at[zs, :, other], ag_s.at[5, zs], ag_r.at[5, zs], mate)

    def quarter(q, start, size):
        return rows.at[pl.ds(pl.multiple_of(q * QUARTER + start, 128), size)]

    def x_copy(i):
        n = 128
        q, start, target = ((x, 0, east), (x, n, west), (x, n, east), (x, 0, west), (xm, 0, east), (xp, n, west))[i]
        return remote(quarter(q, start, n), quarter(q, start, n), x_s.at[i], x_r.at[i], target)

    def x_arrival(i):
        n = 128
        q, start = ((xm, 0), (xp, n), (xm, n), (xp, 0), (x2, 0), (x2, n))[i]
        return remote(quarter(q, start, n), quarter(q, start, n), x_s.at[i], x_r.at[i], mate)

    y_copy(z, True).start()
    y_copy(z, False).start()
    for i in range(4):
        if i != OWN_IN:
            z_copy(i).start()
    for i in range(4):
        x_copy(i).start()

    for i in range(2, 5):
        ready(i)
    logs = jnp.log(row_freq[...].astype(F32)) - total[0]
    row_logs[...] = jnp.broadcast_to(logs, (128, BLOCK)).T

    ids = r * BLOCK + my_rows + lax.broadcasted_iota(jnp.int32, (QUARTER, EXCLUDED), 0)
    listed = jnp.max(jnp.where(ids == excluded[...], 1.0, 0.0), axis=1, keepdims=True)
    root = jnp.sqrt(row_freq[:, pl.ds(my_rows, QUARTER)].astype(F32))
    coef = jnp.broadcast_to(decay_rate * root / (root + 30.0), (128, QUARTER)).T
    decay[...] = jnp.where(listed > 0.0, 0.0, coef)

    def of_block(block, options):
        result = options[3]
        for b in range(3):
            result = lax.select(block == b, options[b], result)
        return result

    def prepare(c):
        h, s = c // 4, lax.rem(c // 2, 2)
        first = lax.rem(c, 2) * HALF
        ref = cnt.at[s, h, pl.ds(first, HALF)]
        pltpu.make_async_copy(ref, ref, cnt_sem.at[c]).wait()
        parity = lax.rem(z + h + FIRST, 2)
        freq = of_block(
            chosen[s],
            [col_freq[:, pl.ds(pl.multiple_of(b * BLOCK + parity * HALF, HALF), HALF)] for b in range(4)],
        )
        col_logs = jnp.log(freq.astype(F32))

        def tile(n, _):
            at = pl.ds(pl.multiple_of(first + n * PIECE, PIECE), PIECE)
            rl = row_logs[at]
            for lane in range(0, HALF, 128):
                count = cnt[s, h, at, lane : lane + 128]
                full = count > 0
                value = jnp.maximum(count, 1).astype(F32)
                root = value * lax.rsqrt(value)
                base[s, h, at, lane : lane + 128] = (rl + col_logs[:, lane : lane + 128]) - jnp.log(value)
                wgt[s, h, at, lane : lane + 128] = jnp.where(
                    full, (0.1 / BLOCK) + (0.25 / BLOCK) * root, 0.0
                )
            return 0

        lax.fori_loop(0, HALF // PIECE, tile, 0)

    def cell_tile(h, n):
        s, q = n // 2, lax.rem(n, 2)
        parity = lax.rem(z + h + FIRST, 2)
        col_tile = of_block(
            chosen[s], [cols[2 * b + parity, pl.ds(2 * q, 2)].reshape(QUARTER, D) for b in range(4)]
        )
        mine[s, h, q] = col_tile
        lane = pl.multiple_of(q * QUARTER, QUARTER)
        for m in range(4):
            at = pl.ds(m * QUARTER, QUARTER)
            predicted = lax.dot_general(
                rows[at], col_tile, (((1,), (1,)), ((), ())), preferred_element_type=F32
            )
            shifted = predicted + base[s, h, at, pl.ds(lane, QUARTER)]
            w = wgt[s, h, at, pl.ds(lane, QUARTER)]
            hinge = 1.0 / (BLOCK + BLOCK * jnp.exp(-shifted))
            cells[s, h, at, pl.ds(lane, QUARTER)] = jnp.where(w > 0.0, w * shifted, hinge).astype(BF16)

    def mate_send(i):
        return remote(part.at[i, :, other], pair_in.at[i], rs_s.at[0, i], rs_r.at[0, i], mate)

    def mate_recv(i):
        return remote(pair_in.at[i], pair_in.at[i], rs_s.at[0, i], rs_r.at[0, i], mate)

    def half_copy(i, up):
        n, target = (0, right) if up else (1, left)
        return remote(send_half.at[n, i], recv_half.at[n, i], rs_s.at[1 + n, i], rs_r.at[1 + n, i], target)

    def full_copy(i, up):
        n, target = (0, right) if up else (1, left)
        return remote(send_full.at[n, i], recv_full.at[n, i], rs_s.at[3 + n, i], rs_r.at[3 + n, i], target)

    def home_copy(i):
        zt = lax.rem(z + pick(i, REDUCE_ORDER), NZ)
        return remote(send_z.at[i], recv_z.at[i], rs_s.at[5, i], rs_r.at[5, i], dev(x, y, zt, k))

    def chip_sum(i, dest):
        return part[i, dest, k] + pair_in[i, dest]

    def col_part(i):
        shift = pick(i, REDUCE_ORDER)
        zt = lax.rem(z + shift, NZ)
        h = lax.rem(shift + FIRST, 2)
        b = zt // 2
        for q in range(2):
            lanes = slice(q * QUARTER, (q + 1) * QUARTER)
            cell = lax.select(chosen[1] == b, cells[1, h, :, lanes], jnp.zeros((BLOCK, QUARTER), BF16))
            found = lax.dot_general(
                lax.select(chosen[0] == b, cells[0, h, :, lanes], cell),
                rows[...],
                (((0,), (0,)), ((), ())),
                preferred_element_type=F32,
            )
            part[i, 2 * q : 2 * q + 2] = found.reshape(2, NK, PIECE, D)

    def row_part(q):
        at = pl.ds(pl.multiple_of(q * QUARTER, QUARTER), QUARTER)
        result = jnp.zeros((QUARTER, D), F32)
        for s in range(2):
            for h in range(2):
                result = result + jnp.dot(
                    cells[s, h, at], mine[s, h].reshape(HALF, D), preferred_element_type=F32
                )
        return result

    def xhalf(up):
        n, target = (0, east) if up else (1, west)
        return remote(xsend_half.at[n], xrecv_half.at[n], x_s.at[6 + n], x_r.at[6 + n], target)

    def xfull(up):
        n, target = (0, east) if up else (1, west)
        return remote(xsend_full.at[n], xrecv_full.at[n], x_s.at[8 + n], x_r.at[8 + n], target)

    lower = PIECE // 2

    def at_step(t, first, count, work):
        @pl.when((t >= first) & (t < first + count))
        def _():
            work(t - first)

    def gather_z(i):
        zs = lax.rem(z + pick(i, GATHER_ORDER), NZ)

        @pl.when(i != OWN_IN)
        def _():
            z_arrival(zs).wait_recv()
            y_copy(zs, True).start()
            y_copy(zs, False).start()

    def gather_more(i):
        @pl.when(4 + i != OWN_IN)
        def _():
            z_copy(4 + i).start()

    def gather_near(i):
        zs = lax.rem(z + pick(i, GATHER_ORDER), NZ)
        y_arrival(zs, True).wait_recv()
        y_forward(zs, True).start()
        y_arrival(zs, False).wait_recv()
        y_forward(zs, False).start()

    def gather_far(i):
        zs = lax.rem(z + pick(i, GATHER_ORDER), NZ)
        y_far(zs, True).wait_recv()
        y_far(zs, False).wait_recv()
        mate_copy(zs).start()

    def gather_rows(_):
        for j in range(2):
            x_arrival(j).wait_recv()
            x_copy(4 + j).start()

    def half_ready(h):
        for j in range(4):
            mate_arrival(lax.rem(z + GATHER_ORDER[4 * h + j], NZ)).wait_recv()

    def rows_ready(_):
        for j in range(2, 6):
            x_arrival(j).wait_recv()

    def prepare_two(i):
        prepare(2 * i)
        prepare(2 * i + 1)

    def two_tiles(h, n):
        cell_tile(h, 2 * n)
        cell_tile(h, 2 * n + 1)

    def reduce_start(i):
        col_part(i)
        mate_send(i).start()

    def reduce_far(j):
        mate_recv(j).wait_recv()
        value = chip_sum(j, y2).astype(BF16)
        send_half[0, j] = value[:lower]
        half_copy(j, True).start()
        send_half[1, j] = value[lower:]
        half_copy(j, False).start()

    def reduce_near(j):
        half_copy(j, True).wait_recv()
        value = chip_sum(j, yp)
        send_full[0, j, :lower] = (value[:lower] + recv_half[0, j].astype(F32)).astype(BF16)
        send_full[0, j, lower:] = value[lower:].astype(BF16)
        full_copy(j, True).start()
        half_copy(j, False).wait_recv()
        value = chip_sum(j, ym)
        send_full[1, j, :lower] = value[:lower].astype(BF16)
        send_full[1, j, lower:] = (value[lower:] + recv_half[1, j].astype(F32)).astype(BF16)
        full_copy(j, False).start()

    def reduce_home(j):
        full_copy(j, True).wait_recv()
        full_copy(j, False).wait_recv()
        value = chip_sum(j, y) + recv_full[0, j].astype(F32) + recv_full[1, j].astype(F32)

        @pl.when(j == OWN_OUT)
        def _():
            col_grad[...] = value

        @pl.when(j != OWN_OUT)
        def _():
            send_z[j] = value.astype(BF16)
            home_copy(j).start()

    def row_far(_):
        value = row_part(x2).astype(BF16)
        xsend_half[0] = value[:128]
        xsend_half[1] = value[128:]
        xhalf(True).start()
        xhalf(False).start()

    def row_east(_):
        value = row_part(xp)
        xhalf(True).wait_recv()
        xsend_full[0, :128] = (value[:128] + xrecv_half[0].astype(F32)).astype(BF16)
        xsend_full[0, 128:] = value[128:].astype(BF16)
        xfull(True).start()

    def row_west(_):
        value = row_part(xm)
        xhalf(False).wait_recv()
        xsend_full[1, :128] = value[:128].astype(BF16)
        xsend_full[1, 128:] = (value[128:] + xrecv_half[1].astype(F32)).astype(BF16)
        xfull(False).start()

    def row_own(_):
        own_grad[...] = row_part(x)

    def result_copy(i):
        at = pl.ds((0, 2 * QUARTER)[i], (2 * QUARTER, 2 * PIECE)[i])
        return pltpu.make_async_copy(made.at[at], result.at[at], cnt_sem.at[10 + i])

    def row_update(_):
        sums_copy(0).wait()
        xfull(True).wait_recv()
        xfull(False).wait_recv()
        for lane in range(0, D, 128):
            at = slice(lane, lane + 128)
            value = row_local[:, at]
            grad = own_grad[:, at] + xrecv_full[0, :, at].astype(F32) + xrecv_full[1, :, at].astype(F32)
            grad = grad + decay[...] * value
            sums = row_sums[:, at] + grad * grad
            made[:QUARTER, at] = value - learn_rate * grad * lax.rsqrt(sums)
            made[QUARTER : 2 * QUARTER, at] = sums
        result_copy(0).start()

    def step(t, _):
        at_step(t, 0, 8, gather_z)
        at_step(t, GATHER_MORE, 4, gather_more)
        at_step(t, GATHER_NEAR, 8, gather_near)
        at_step(t, GATHER_FAR, 8, gather_far)
        at_step(t, 2, 1, gather_rows)
        at_step(t, REDUCE, 8, reduce_start)
        at_step(t, REDUCE_HOME, 8, reduce_home)
        at_step(t, REDUCE_NEAR, 8, reduce_near)
        at_step(t, REDUCE_FAR, 8, reduce_far)
        at_step(t, 0, 4, prepare_two)
        at_step(t, CELLS, 1, rows_ready)
        at_step(t, CELLS, 1, lambda _: half_ready(0))
        at_step(t, CELLS, 2, lambda n: two_tiles(0, n))
        at_step(t, CELLS_MORE, 1, lambda _: half_ready(1))
        at_step(t, CELLS_MORE, 2, lambda n: two_tiles(1, n))
        at_step(t, ROWS, 1, row_far)
        at_step(t, ROWS + 1, 1, row_east)
        at_step(t, ROWS + 2, 1, row_west)
        at_step(t, ROWS + 3, 1, row_own)
        at_step(t, ROWS + 6, 1, row_update)
        return 0

    lax.fori_loop(0, REDUCE_HOME + 8, step, 0)
    sums_copy(1).wait()
    for j in OTHERS:
        home_copy(j).wait_recv()
    for lane in range(0, D, 128):
        at = slice(lane, lane + 128)
        grad = col_grad[:, at]
        for j in OTHERS:
            grad = grad + recv_z[j, :, at].astype(F32)
        sums = col_sums[:, at] + grad * grad
        made[2 * QUARTER : 2 * QUARTER + PIECE, at] = (
            col_local[:, at] - learn_rate * grad * lax.rsqrt(sums)
        )
        made[2 * QUARTER + PIECE :, at] = sums
    result_copy(1).start()

    for j in range(NZ):
        if j != OWN_IN:
            z_copy(j).wait_send()

    def drain(j, _):
        for up in (True, False):
            y_copy(j, up).wait_send()
            y_forward(j, up).wait_send()
            half_copy(j, up).wait_send()
            full_copy(j, up).wait_send()
        mate_copy(j).wait_send()
        mate_send(j).wait_send()

        @pl.when(j != OWN_OUT)
        def _():
            home_copy(j).wait_send()

        return 0

    lax.fori_loop(0, NZ, drain, 0)
    for j in range(6):
        x_copy(j).wait_send()
    for up in (True, False):
        xhalf(up).wait_send()
        xfull(up).wait_send()
    for i in range(2):
        result_copy(i).wait()


def split_kernel(result, row_new, row_accum_new, col_new, col_accum_new, held, sem):
    reads, writes = [], []
    first = 0
    for i, out in enumerate((row_new, row_accum_new, col_new, col_accum_new)):
        at = pl.ds(first, out.shape[0])
        reads.append(pltpu.make_async_copy(result.at[at], held.at[at], sem.at[i]))
        writes.append(pltpu.make_async_copy(held.at[at], out, sem.at[4 + i]))
        first += out.shape[0]
    for read in reads:
        read.start()
    for read, write in zip(reads, writes):
        read.wait()
        write.start()
    for write in writes:
        write.wait()


def body(
    row_embed,
    row_accum,
    col_embed,
    col_accum,
    col_freq,
    row_freq,
    block_cols,
    counts,
    excluded,
    log_total,
):
    smem = pl.BlockSpec(memory_space=pltpu.SMEM)
    hbm = pl.BlockSpec(memory_space=pl.ANY)
    row_shape = jax.ShapeDtypeStruct((QUARTER, D), F32)
    col_shape = jax.ShapeDtypeStruct((PIECE, D), F32)
    result = pl.pallas_call(
        step_kernel,
        out_shape=jax.ShapeDtypeStruct((2 * QUARTER + 2 * PIECE, D), F32),
        in_specs=[smem, smem] + [hbm] * 8,
        out_specs=hbm,
        scratch_shapes=[
            pltpu.VMEM((QUARTER, D), F32),
            pltpu.VMEM((PIECE, D), F32),
            pltpu.VMEM((1, BLOCK), jnp.int32),
            pltpu.VMEM((1, NY * BLOCK), jnp.int32),
            pltpu.VMEM((1, EXCLUDED), jnp.int32),
            pltpu.VMEM((2 * QUARTER + 2 * PIECE, D), F32),
            pltpu.VMEM((QUARTER, D), F32),
            pltpu.VMEM((PIECE, D), F32),
            pltpu.VMEM((QUARTER, D), F32),
            pltpu.VMEM((PIECE, D), F32),
            pltpu.VMEM((QUARTER, 128), F32),
            pltpu.VMEM((NZ, NY, NK, PIECE, D), BF16),
            pltpu.VMEM((2, 2, 2, QUARTER, D), BF16),
            pltpu.VMEM((BLOCK, D), BF16),
            pltpu.VMEM((2, 2, BLOCK, HALF), jnp.int32),
            pltpu.VMEM((2, 2, BLOCK, HALF), F32),
            pltpu.VMEM((2, 2, BLOCK, HALF), F32),
            pltpu.VMEM((2, 2, BLOCK, HALF), BF16),
            pltpu.VMEM((BLOCK, 128), F32),
            pltpu.VMEM((NZ, NY, NK, PIECE, D), F32),
            pltpu.VMEM((NZ, NY, PIECE, D), F32),
            pltpu.VMEM((2, NZ, PIECE // 2, D), BF16),
            pltpu.VMEM((2, NZ, PIECE // 2, D), BF16),
            pltpu.VMEM((2, NZ, PIECE, D), BF16),
            pltpu.VMEM((2, NZ, PIECE, D), BF16),
            pltpu.VMEM((NZ, PIECE, D), BF16),
            pltpu.VMEM((NZ, PIECE, D), BF16),
            pltpu.VMEM((2, 128, D), BF16),
            pltpu.VMEM((2, 128, D), BF16),
            pltpu.VMEM((2, QUARTER, D), BF16),
            pltpu.VMEM((2, QUARTER, D), BF16),
            pltpu.SemaphoreType.DMA((17,)),
            pltpu.SemaphoreType.DMA((6, NZ)),
            pltpu.SemaphoreType.DMA((6, NZ)),
            pltpu.SemaphoreType.DMA((6, NZ)),
            pltpu.SemaphoreType.DMA((6, NZ)),
            pltpu.SemaphoreType.DMA((10,)),
            pltpu.SemaphoreType.DMA((10,)),
        ],
        compiler_params=pltpu.CompilerParams(
            collective_id=0, has_side_effects=True, vmem_limit_bytes=58 << 20
        ),
        cost_estimate=pl.CostEstimate(
            flops=8 << 30, bytes_accessed=12 << 20, transcendentals=8 << 20
        ),
        name="swivel_step",
    )(
        block_cols.reshape(2),
        log_total.reshape(1),
        row_embed,
        col_embed[0],
        row_freq.reshape(1, BLOCK),
        col_freq,
        excluded.reshape(1, EXCLUDED),
        row_accum,
        col_accum[0],
        counts[0, 0],
    )
    row_new, row_accum_new, col_new, col_accum_new = pl.pallas_call(
        split_kernel,
        out_shape=(row_shape, row_shape, col_shape, col_shape),
        in_specs=[hbm],
        out_specs=(hbm, hbm, hbm, hbm),
        scratch_shapes=[
            pltpu.VMEM((2 * QUARTER + 2 * PIECE, D), F32),
            pltpu.SemaphoreType.DMA((8,)),
        ],
        name="split_result",
    )(result)
    return (row_new, row_accum_new, col_new[None], col_accum_new[None])


def solution(mesh):
    in_specs = (
        P(("row", "col"), None),
        P(("row", "col"), None),
        P("col", "row", None),
        P("col", "row", None),
        P("col", None),
        P("row"),
        P("row", "col", None),
        P("row", "col", None, None, None),
        P(),
        P(),
    )
    out_specs = (
        P(("row", "col"), None),
        P(("row", "col"), None),
        P("col", "row", None),
        P("col", "row", None),
    )
    return jax.shard_map(body, mesh=mesh, in_specs=in_specs, out_specs=out_specs, check_vma=False)
```

```python
import jax
import jax.numpy as jnp
from jax import lax
from jax.experimental import pallas as pl
from jax.experimental.pallas import tpu as pltpu
from jax.sharding import PartitionSpec as P

MESH = pl.DeviceIdType.MESH
NX, NY, NZ, NK = 4, 4, 8, 2
BLOCK = 1024
HALF = 512
EXCLUDED = 512
PIECE = 64
QUARTER = 256
D = 512
F32 = jnp.float32
BF16 = jnp.bfloat16

learn_rate = 0.2
decay_rate = 0.5

GATHER_ORDER = (1, 7, 3, 5, 0, 2, 6, 4)
REDUCE_ORDER = (3, 5, 1, 7, 4, 2, 6, 0)
OWN_IN = GATHER_ORDER.index(0)
OWN_OUT = REDUCE_ORDER.index(0)
FIRST = GATHER_ORDER[1] % 2
OTHERS = tuple(j for j in range(NZ) if j != OWN_OUT)

GATHER_MORE = 1
GATHER_NEAR = 2
GATHER_FAR = 4
CELLS = 8
REDUCE = 10
CELLS_MORE = REDUCE + 2
REDUCE_FAR = REDUCE + 2
REDUCE_NEAR = REDUCE + 4
REDUCE_HOME = REDUCE + 6
ROWS = REDUCE + 5


def pick(index, values):
    result = jnp.int32(values[-1])
    for place in range(len(values) - 1):
        result = jnp.where(index == place, jnp.int32(values[place]), result)
    return result


def step_kernel(
    chosen, total, row_in, col_in, row_freq_in, col_freq_in, excluded_in, row_accum, col_accum, counts,
    result,
    row_local, col_local, row_freq, col_freq, excluded,
    made, own_grad, col_grad, row_sums, col_sums, decay,
    cols, mine, rows, cnt, wgt, base, cells, row_logs,
    part, pair_in, send_half, recv_half, send_full, recv_full, send_z, recv_z,
    xsend_half, xrecv_half, xsend_full, xrecv_full,
    cnt_sem, ag_s, ag_r, rs_s, rs_r, x_s, x_r,
):
    r = lax.axis_index("row")
    x = lax.axis_index("col")
    k = lax.rem(r, NK)
    y = lax.rem(r // NK, NY)
    z = r // (NK * NY)
    yp, ym, y2 = lax.rem(y + 1, NY), lax.rem(y + 3, NY), lax.rem(y + 2, NY)
    xp, xm, x2 = lax.rem(x + 1, NX), lax.rem(x + 3, NX), lax.rem(x + 2, NX)
    other = 1 - k

    def dev(dx, dy, dz, dk):
        return ((dz * NY + dy) * NK + dk, dx)

    right, left = dev(x, yp, z, k), dev(x, ym, z, k)
    east, west = dev(xp, y, z, k), dev(xm, y, z, k)
    mate = dev(x, y, z, other)

    def remote(src, dst, s, q, target):
        return pltpu.make_async_remote_copy(
            src_ref=src, dst_ref=dst, send_sem=s, recv_sem=q, device_id=target, device_id_type=MESH
        )

    def count_copy(c):
        h, s, b = c // 4, (c // 2) % 2, c % 2
        lane = pl.multiple_of(lax.rem(z + h + FIRST, 2) * HALF, HALF)
        return pltpu.make_async_copy(
            counts.at[s, pl.ds(b * HALF, HALF), pl.ds(lane, HALF)],
            cnt.at[s, h, pl.ds(b * HALF, HALF)],
            cnt_sem.at[c],
        )

    def sums_copy(i):
        return pltpu.make_async_copy(
            (row_accum, col_accum)[i], (row_sums, col_sums)[i], cnt_sem.at[8 + i]
        )

    barrier = pltpu.get_barrier_semaphore()
    for target in (right, left, east, west, mate):
        pl.semaphore_signal(barrier, inc=1, device_id=target, device_id_type=MESH)
    for dz in range(1, NZ):
        pl.semaphore_signal(
            barrier, inc=1, device_id=dev(x, y, lax.rem(z + dz, NZ), k), device_id_type=MESH
        )
    sources = (col_in, row_in, row_freq_in, col_freq_in, excluded_in)
    targets = (col_local, row_local, row_freq, col_freq, excluded)
    for i in range(5):
        pltpu.make_async_copy(sources[i], targets[i], cnt_sem.at[12 + i]).start()

    for c in range(8):
        count_copy(c).start()
    for i in range(2):
        sums_copy(i).start()

    def ready(i):
        pltpu.make_async_copy(sources[i], targets[i], cnt_sem.at[12 + i]).wait()

    ready(0)
    cols[z, y, k] = col_local[...].astype(BF16)
    my_rows = pl.multiple_of(x * QUARTER, QUARTER)
    ready(1)
    rows[pl.ds(my_rows, QUARTER)] = row_local[...].astype(BF16)
    pl.semaphore_wait(barrier, 5 + NZ - 1)

    def z_copy(i):
        zt = lax.rem(z + pick(i, GATHER_ORDER), NZ)
        return remote(cols.at[z, y, k], cols.at[z, y, k], ag_s.at[0, i], ag_r.at[0, z], dev(x, y, zt, k))

    def z_arrival(zs):
        return remote(cols.at[zs, y, k], cols.at[zs, y, k], ag_s.at[0, 0], ag_r.at[0, zs], mate)

    def y_copy(zs, up):
        kind, target = (1, right) if up else (2, left)
        return remote(cols.at[zs, y, k], cols.at[zs, y, k], ag_s.at[kind, zs], ag_r.at[kind, zs], target)

    def y_arrival(zs, up):
        kind, src = (1, ym) if up else (2, yp)
        return remote(cols.at[zs, src, k], cols.at[zs, src, k], ag_s.at[kind, zs], ag_r.at[kind, zs], mate)

    def y_forward(zs, up):
        kind, src, start, target = (3, ym, 0, right) if up else (4, yp, PIECE // 2, left)
        ref = cols.at[zs, src, k, pl.ds(start, PIECE // 2)]
        return remote(ref, ref, ag_s.at[kind, zs], ag_r.at[kind, zs], target)

    def y_far(zs, up):
        kind, start = (3, 0) if up else (4, PIECE // 2)
        ref = cols.at[zs, y2, k, pl.ds(start, PIECE // 2)]
        return remote(ref, ref, ag_s.at[kind, zs], ag_r.at[kind, zs], mate)

    def mate_copy(zs):
        return remote(cols.at[zs, :, k], cols.at[zs, :, k], ag_s.at[5, zs], ag_r.at[5, zs], mate)

    def mate_arrival(zs):
        return remote(cols.at[zs, :, other], cols.at[zs, :, other], ag_s.at[5, zs], ag_r.at[5, zs], mate)

    def quarter(q, start, size):
        return rows.at[pl.ds(pl.multiple_of(q * QUARTER + start, 128), size)]

    def x_copy(i):
        n = 128
        q, start, target = ((x, 0, east), (x, n, west), (x, n, east), (x, 0, west), (xm, 0, east), (xp, n, west))[i]
        return remote(quarter(q, start, n), quarter(q, start, n), x_s.at[i], x_r.at[i], target)

    def x_arrival(i):
        n = 128
        q, start = ((xm, 0), (xp, n), (xm, n), (xp, 0), (x2, 0), (x2, n))[i]
        return remote(quarter(q, start, n), quarter(q, start, n), x_s.at[i], x_r.at[i], mate)

    y_copy(z, True).start()
    y_copy(z, False).start()
    for i in range(4):
        if i != OWN_IN:
            z_copy(i).start()
    for i in range(4):
        x_copy(i).start()

    for i in range(2, 5):
        ready(i)
    logs = jnp.log(row_freq[...].astype(F32)) - total[0]
    row_logs[...] = jnp.broadcast_to(logs, (128, BLOCK)).T

    ids = r * BLOCK + my_rows + lax.broadcasted_iota(jnp.int32, (QUARTER, EXCLUDED), 0)
    listed = jnp.max(jnp.where(ids == excluded[...], 1.0, 0.0), axis=1, keepdims=True)
    root = jnp.sqrt(row_freq[:, pl.ds(my_rows, QUARTER)].astype(F32))
    coef = jnp.broadcast_to(decay_rate * root / (root + 30.0), (128, QUARTER)).T
    decay[...] = jnp.where(listed > 0.0, 0.0, coef)

    def of_block(block, options):
        result = options[3]
        for b in range(3):
            result = lax.select(block == b, options[b], result)
        return result

    def prepare(c):
        h, s = c // 4, lax.rem(c // 2, 2)
        first = lax.rem(c, 2) * HALF
        ref = cnt.at[s, h, pl.ds(first, HALF)]
        pltpu.make_async_copy(ref, ref, cnt_sem.at[c]).wait()
        parity = lax.rem(z + h + FIRST, 2)
        freq = of_block(
            chosen[s],
            [col_freq[:, pl.ds(pl.multiple_of(b * BLOCK + parity * HALF, HALF), HALF)] for b in range(4)],
        )
        col_logs = jnp.log(freq.astype(F32))

        def tile(n, _):
            at = pl.ds(pl.multiple_of(first + n * PIECE, PIECE), PIECE)
            rl = row_logs[at]
            for lane in range(0, HALF, 128):
                count = cnt[s, h, at, lane : lane + 128]
                full = count > 0
                value = jnp.maximum(count, 1).astype(F32)
                root = value * lax.rsqrt(value)
                base[s, h, at, lane : lane + 128] = (rl + col_logs[:, lane : lane + 128]) - jnp.log(value)
                wgt[s, h, at, lane : lane + 128] = jnp.where(
                    full, (0.1 / BLOCK) + (0.25 / BLOCK) * root, 0.0
                )
            return 0

        lax.fori_loop(0, HALF // PIECE, tile, 0)

    def cell_tile(h, n):
        s, q = n // 2, lax.rem(n, 2)
        parity = lax.rem(z + h + FIRST, 2)
        col_tile = of_block(
            chosen[s], [cols[2 * b + parity, pl.ds(2 * q, 2)].reshape(QUARTER, D) for b in range(4)]
        )
        mine[s, h, q] = col_tile
        lane = pl.multiple_of(q * QUARTER, QUARTER)
        for m in range(4):
            at = pl.ds(m * QUARTER, QUARTER)
            predicted = lax.dot_general(
                rows[at], col_tile, (((1,), (1,)), ((), ())), preferred_element_type=F32
            )
            shifted = predicted + base[s, h, at, pl.ds(lane, QUARTER)]
            w = wgt[s, h, at, pl.ds(lane, QUARTER)]
            hinge = 1.0 / (BLOCK + BLOCK * jnp.exp(-shifted))
            cells[s, h, at, pl.ds(lane, QUARTER)] = jnp.where(w > 0.0, w * shifted, hinge).astype(BF16)

    def mate_send(i):
        return remote(part.at[i, :, other], pair_in.at[i], rs_s.at[0, i], rs_r.at[0, i], mate)

    def mate_recv(i):
        return remote(pair_in.at[i], pair_in.at[i], rs_s.at[0, i], rs_r.at[0, i], mate)

    def half_copy(i, up):
        n, target = (0, right) if up else (1, left)
        return remote(send_half.at[n, i], recv_half.at[n, i], rs_s.at[1 + n, i], rs_r.at[1 + n, i], target)

    def full_copy(i, up):
        n, target = (0, right) if up else (1, left)
        return remote(send_full.at[n, i], recv_full.at[n, i], rs_s.at[3 + n, i], rs_r.at[3 + n, i], target)

    def home_copy(i):
        zt = lax.rem(z + pick(i, REDUCE_ORDER), NZ)
        return remote(send_z.at[i], recv_z.at[i], rs_s.at[5, i], rs_r.at[5, i], dev(x, y, zt, k))

    def chip_sum(i, dest):
        return part[i, dest, k] + pair_in[i, dest]

    def col_part(i):
        shift = pick(i, REDUCE_ORDER)
        zt = lax.rem(z + shift, NZ)
        h = lax.rem(shift + FIRST, 2)
        b = zt // 2
        for q in range(2):
            lanes = slice(q * QUARTER, (q + 1) * QUARTER)
            cell = lax.select(chosen[1] == b, cells[1, h, :, lanes], jnp.zeros((BLOCK, QUARTER), BF16))
            found = lax.dot_general(
                lax.select(chosen[0] == b, cells[0, h, :, lanes], cell),
                rows[...],
                (((0,), (0,)), ((), ())),
                preferred_element_type=F32,
            )
            part[i, 2 * q : 2 * q + 2] = found.reshape(2, NK, PIECE, D)

    def row_part(q):
        at = pl.ds(pl.multiple_of(q * QUARTER, QUARTER), QUARTER)
        result = jnp.zeros((QUARTER, D), F32)
        for s in range(2):
            for h in range(2):
                result = result + jnp.dot(
                    cells[s, h, at], mine[s, h].reshape(HALF, D), preferred_element_type=F32
                )
        return result

    def xhalf(up):
        n, target = (0, east) if up else (1, west)
        return remote(xsend_half.at[n], xrecv_half.at[n], x_s.at[6 + n], x_r.at[6 + n], target)

    def xfull(up):
        n, target = (0, east) if up else (1, west)
        return remote(xsend_full.at[n], xrecv_full.at[n], x_s.at[8 + n], x_r.at[8 + n], target)

    lower = PIECE // 2

    def at_step(t, first, count, work):
        @pl.when((t >= first) & (t < first + count))
        def _():
            work(t - first)

    def gather_z(i):
        zs = lax.rem(z + pick(i, GATHER_ORDER), NZ)

        @pl.when(i != OWN_IN)
        def _():
            z_arrival(zs).wait_recv()
            y_copy(zs, True).start()
            y_copy(zs, False).start()

    def gather_more(i):
        @pl.when(4 + i != OWN_IN)
        def _():
            z_copy(4 + i).start()

    def gather_near(i):
        zs = lax.rem(z + pick(i, GATHER_ORDER), NZ)
        y_arrival(zs, True).wait_recv()
        y_forward(zs, True).start()
        y_arrival(zs, False).wait_recv()
        y_forward(zs, False).start()

    def gather_far(i):
        zs = lax.rem(z + pick(i, GATHER_ORDER), NZ)
        y_far(zs, True).wait_recv()
        y_far(zs, False).wait_recv()
        mate_copy(zs).start()

    def gather_rows(_):
        for j in range(2):
            x_arrival(j).wait_recv()
            x_copy(4 + j).start()

    def half_ready(h):
        for j in range(4):
            mate_arrival(lax.rem(z + GATHER_ORDER[4 * h + j], NZ)).wait_recv()

    def rows_ready(_):
        for j in range(2, 6):
            x_arrival(j).wait_recv()

    def prepare_two(i):
        prepare(2 * i)
        prepare(2 * i + 1)

    def two_tiles(h, n):
        cell_tile(h, 2 * n)
        cell_tile(h, 2 * n + 1)

    def reduce_start(i):
        col_part(i)
        mate_send(i).start()

    def reduce_far(j):
        mate_recv(j).wait_recv()
        value = chip_sum(j, y2).astype(BF16)
        send_half[0, j] = value[:lower]
        half_copy(j, True).start()
        send_half[1, j] = value[lower:]
        half_copy(j, False).start()

    def reduce_near(j):
        half_copy(j, True).wait_recv()
        value = chip_sum(j, yp)
        send_full[0, j, :lower] = (value[:lower] + recv_half[0, j].astype(F32)).astype(BF16)
        send_full[0, j, lower:] = value[lower:].astype(BF16)
        full_copy(j, True).start()
        half_copy(j, False).wait_recv()
        value = chip_sum(j, ym)
        send_full[1, j, :lower] = value[:lower].astype(BF16)
        send_full[1, j, lower:] = (value[lower:] + recv_half[1, j].astype(F32)).astype(BF16)
        full_copy(j, False).start()

    def reduce_home(j):
        full_copy(j, True).wait_recv()
        full_copy(j, False).wait_recv()
        value = chip_sum(j, y) + recv_full[0, j].astype(F32) + recv_full[1, j].astype(F32)

        @pl.when(j == OWN_OUT)
        def _():
            col_grad[...] = value

        @pl.when(j != OWN_OUT)
        def _():
            send_z[j] = value.astype(BF16)
            home_copy(j).start()

    def row_far(_):
        value = row_part(x2).astype(BF16)
        xsend_half[0] = value[:128]
        xsend_half[1] = value[128:]
        xhalf(True).start()
        xhalf(False).start()

    def row_east(_):
        value = row_part(xp)
        xhalf(True).wait_recv()
        xsend_full[0, :128] = (value[:128] + xrecv_half[0].astype(F32)).astype(BF16)
        xsend_full[0, 128:] = value[128:].astype(BF16)
        xfull(True).start()

    def row_west(_):
        value = row_part(xm)
        xhalf(False).wait_recv()
        xsend_full[1, :128] = value[:128].astype(BF16)
        xsend_full[1, 128:] = (value[128:] + xrecv_half[1].astype(F32)).astype(BF16)
        xfull(False).start()

    def row_own(_):
        own_grad[...] = row_part(x)

    def result_copy(i):
        at = pl.ds((0, 2 * QUARTER)[i], (2 * QUARTER, 2 * PIECE)[i])
        return pltpu.make_async_copy(made.at[at], result.at[at], cnt_sem.at[10 + i])

    def row_update(_):
        sums_copy(0).wait()
        xfull(True).wait_recv()
        xfull(False).wait_recv()
        for lane in range(0, D, 128):
            at = slice(lane, lane + 128)
            value = row_local[:, at]
            grad = own_grad[:, at] + xrecv_full[0, :, at].astype(F32) + xrecv_full[1, :, at].astype(F32)
            grad = grad + decay[...] * value
            sums = row_sums[:, at] + grad * grad
            made[:QUARTER, at] = value - learn_rate * grad * lax.rsqrt(sums)
            made[QUARTER : 2 * QUARTER, at] = sums
        result_copy(0).start()

    def step(t, _):
        at_step(t, 0, 8, gather_z)
        at_step(t, GATHER_MORE, 4, gather_more)
        at_step(t, 0, 4, prepare_two)
        at_step(t, GATHER_NEAR, 8, gather_near)
        at_step(t, GATHER_FAR, 8, gather_far)
        at_step(t, 2, 1, gather_rows)
        at_step(t, REDUCE, 8, reduce_start)
        at_step(t, REDUCE_HOME, 8, reduce_home)
        at_step(t, REDUCE_NEAR, 8, reduce_near)
        at_step(t, REDUCE_FAR, 8, reduce_far)
        at_step(t, CELLS, 1, rows_ready)
        at_step(t, CELLS, 1, lambda _: half_ready(0))
        at_step(t, CELLS, 2, lambda n: two_tiles(0, n))
        at_step(t, CELLS_MORE, 1, lambda _: half_ready(1))
        at_step(t, CELLS_MORE, 2, lambda n: two_tiles(1, n))
        at_step(t, ROWS, 1, row_far)
        at_step(t, ROWS + 1, 1, row_east)
        at_step(t, ROWS + 2, 1, row_west)
        at_step(t, ROWS + 3, 1, row_own)
        at_step(t, ROWS + 6, 1, row_update)
        return 0

    lax.fori_loop(0, REDUCE_HOME + 8, step, 0)
    sums_copy(1).wait()
    for j in OTHERS:
        home_copy(j).wait_recv()
    for lane in range(0, D, 128):
        at = slice(lane, lane + 128)
        grad = col_grad[:, at]
        for j in OTHERS:
            grad = grad + recv_z[j, :, at].astype(F32)
        sums = col_sums[:, at] + grad * grad
        made[2 * QUARTER : 2 * QUARTER + PIECE, at] = (
            col_local[:, at] - learn_rate * grad * lax.rsqrt(sums)
        )
        made[2 * QUARTER + PIECE :, at] = sums
    result_copy(1).start()

    for j in range(NZ):
        if j != OWN_IN:
            z_copy(j).wait_send()

    def drain(j, _):
        for up in (True, False):
            y_copy(j, up).wait_send()
            y_forward(j, up).wait_send()
            half_copy(j, up).wait_send()
            full_copy(j, up).wait_send()
        mate_copy(j).wait_send()
        mate_send(j).wait_send()

        @pl.when(j != OWN_OUT)
        def _():
            home_copy(j).wait_send()

        return 0

    lax.fori_loop(0, NZ, drain, 0)
    for j in range(6):
        x_copy(j).wait_send()
    for up in (True, False):
        xhalf(up).wait_send()
        xfull(up).wait_send()
    for i in range(2):
        result_copy(i).wait()


def split_kernel(result, row_new, row_accum_new, col_new, col_accum_new, held, sem):
    reads, writes = [], []
    first = 0
    for i, out in enumerate((row_new, row_accum_new, col_new, col_accum_new)):
        at = pl.ds(first, out.shape[0])
        reads.append(pltpu.make_async_copy(result.at[at], held.at[at], sem.at[i]))
        writes.append(pltpu.make_async_copy(held.at[at], out, sem.at[4 + i]))
        first += out.shape[0]
    for read in reads:
        read.start()
    for read, write in zip(reads, writes):
        read.wait()
        write.start()
    for write in writes:
        write.wait()


def body(
    row_embed,
    row_accum,
    col_embed,
    col_accum,
    col_freq,
    row_freq,
    block_cols,
    counts,
    excluded,
    log_total,
):
    smem = pl.BlockSpec(memory_space=pltpu.SMEM)
    hbm = pl.BlockSpec(memory_space=pl.ANY)
    row_shape = jax.ShapeDtypeStruct((QUARTER, D), F32)
    col_shape = jax.ShapeDtypeStruct((PIECE, D), F32)
    result = pl.pallas_call(
        step_kernel,
        out_shape=jax.ShapeDtypeStruct((2 * QUARTER + 2 * PIECE, D), F32),
        in_specs=[smem, smem] + [hbm] * 8,
        out_specs=hbm,
        scratch_shapes=[
            pltpu.VMEM((QUARTER, D), F32),
            pltpu.VMEM((PIECE, D), F32),
            pltpu.VMEM((1, BLOCK), jnp.int32),
            pltpu.VMEM((1, NY * BLOCK), jnp.int32),
            pltpu.VMEM((1, EXCLUDED), jnp.int32),
            pltpu.VMEM((2 * QUARTER + 2 * PIECE, D), F32),
            pltpu.VMEM((QUARTER, D), F32),
            pltpu.VMEM((PIECE, D), F32),
            pltpu.VMEM((QUARTER, D), F32),
            pltpu.VMEM((PIECE, D), F32),
            pltpu.VMEM((QUARTER, 128), F32),
            pltpu.VMEM((NZ, NY, NK, PIECE, D), BF16),
            pltpu.VMEM((2, 2, 2, QUARTER, D), BF16),
            pltpu.VMEM((BLOCK, D), BF16),
            pltpu.VMEM((2, 2, BLOCK, HALF), jnp.int32),
            pltpu.VMEM((2, 2, BLOCK, HALF), F32),
            pltpu.VMEM((2, 2, BLOCK, HALF), F32),
            pltpu.VMEM((2, 2, BLOCK, HALF), BF16),
            pltpu.VMEM((BLOCK, 128), F32),
            pltpu.VMEM((NZ, NY, NK, PIECE, D), F32),
            pltpu.VMEM((NZ, NY, PIECE, D), F32),
            pltpu.VMEM((2, NZ, PIECE // 2, D), BF16),
            pltpu.VMEM((2, NZ, PIECE // 2, D), BF16),
            pltpu.VMEM((2, NZ, PIECE, D), BF16),
            pltpu.VMEM((2, NZ, PIECE, D), BF16),
            pltpu.VMEM((NZ, PIECE, D), BF16),
            pltpu.VMEM((NZ, PIECE, D), BF16),
            pltpu.VMEM((2, 128, D), BF16),
            pltpu.VMEM((2, 128, D), BF16),
            pltpu.VMEM((2, QUARTER, D), BF16),
            pltpu.VMEM((2, QUARTER, D), BF16),
            pltpu.SemaphoreType.DMA((17,)),
            pltpu.SemaphoreType.DMA((6, NZ)),
            pltpu.SemaphoreType.DMA((6, NZ)),
            pltpu.SemaphoreType.DMA((6, NZ)),
            pltpu.SemaphoreType.DMA((6, NZ)),
            pltpu.SemaphoreType.DMA((10,)),
            pltpu.SemaphoreType.DMA((10,)),
        ],
        compiler_params=pltpu.CompilerParams(
            collective_id=0, has_side_effects=True, vmem_limit_bytes=58 << 20
        ),
        cost_estimate=pl.CostEstimate(
            flops=8 << 30, bytes_accessed=12 << 20, transcendentals=8 << 20
        ),
        name="swivel_step",
    )(
        block_cols.reshape(2),
        log_total.reshape(1),
        row_embed,
        col_embed[0],
        row_freq.reshape(1, BLOCK),
        col_freq,
        excluded.reshape(1, EXCLUDED),
        row_accum,
        col_accum[0],
        counts[0, 0],
    )
    row_new, row_accum_new, col_new, col_accum_new = pl.pallas_call(
        split_kernel,
        out_shape=(row_shape, row_shape, col_shape, col_shape),
        in_specs=[hbm],
        out_specs=(hbm, hbm, hbm, hbm),
        scratch_shapes=[
            pltpu.VMEM((2 * QUARTER + 2 * PIECE, D), F32),
            pltpu.SemaphoreType.DMA((8,)),
        ],
        name="split_result",
    )(result)
    return (row_new, row_accum_new, col_new[None], col_accum_new[None])


def solution(mesh):
    in_specs = (
        P(("row", "col"), None),
        P(("row", "col"), None),
        P("col", "row", None),
        P("col", "row", None),
        P("col", None),
        P("row"),
        P("row", "col", None),
        P("row", "col", None, None, None),
        P(),
        P(),
    )
    out_specs = (
        P(("row", "col"), None),
        P(("row", "col"), None),
        P("col", "row", None),
        P("col", "row", None),
    )
    return jax.shard_map(body, mesh=mesh, in_specs=in_specs, out_specs=out_specs, check_vma=False)
```
